512 devices in a mesh: dp: 32 (over x, y), tile: 16 (over z, core).
Axes of the slice: x: 4, y: 8, z: 8, core: 2. Of those that a mesh axis runs over, the one named last changes fastest.
Arguments:
- inputs: bfloat16 [32, 32, 512, 256], P('dp', None, 'tile'), may hold values from -6 to 6
- kernel: bfloat16 [2304, 256], replicated, may hold values from -0.125 to 0.125
- cotangent: bfloat16 [32, 32, 512, 256], P('dp', None, 'tile'), may hold values from -6 to 6
- feedback: float32 [32, 2304, 256], P('dp', 'tile'), may hold values from -4 to 4
- q_start: float32 [256, 8], replicated, may hold values from -6 to 6
Outputs:
- output: bfloat16 [32, 32, 512, 256], P('dp', None, 'tile')
- input_grad: bfloat16 [32, 32, 512, 256], P('dp', None, 'tile')
- p_factor: float32 [2304, 8], P('tile')
- q_factor: float32 [256, 8], replicated
- new_feedback: float32 [32, 2304, 256], P('dp', 'tile')
The draws below stay inside these ranges and needn't reach their ends.
All inputs are finite; a program needn't handle non-finite values.
Results may differ from the reference program's by a relative error of at most 0.017.
Values may be sent and summed in bfloat16 or wider, within the bound.
No kernel may reach another device: no remote copies, remote signals or barrier semaphores. Data moves between devices by JAX's collectives and lax.ppermute only.
A program may use at most 64 MiB of HBM per device.

```python
import math
import jax
import jax.numpy as jnp
from jax import lax

CH = 256
RANK = 8
LAT = 32
LON = 512
KROWS = 2304
IMAGES = 32
N_DP = 32


def level_of(rng, shape, cuts, low, high):
    factor_of = 1.0
    for dim, shards_of in cuts:
        steps = jax.random.uniform(jax.random.fold_in(jax.random.fold_in(rng, 6), dim), (shards_of,), jnp.float32, low / len(cuts), high / len(cuts))
        factor_of = factor_of * jnp.repeat(jnp.exp(steps), shape[dim] // shards_of).reshape((-1,) + (1,) * (len(shape) - 1 - dim))
    return factor_of


def centred(stream_key, dims, scale, reach, cuts=(), kind=jnp.bfloat16):
    array = jax.random.normal(stream_key, dims, jnp.float32) * scale
    if len(cuts) > 0:
        array = level_of(stream_key, dims, cuts, -0.22, 0.18) * array
    return jnp.clip(array, min=-reach, max=reach).astype(kind)


def setup_inputs(seed: int = 0) -> dict:
    key_of = jax.random.split(jax.random.key(seed), 6)
    return {
        "inputs": centred(key_of[0], (IMAGES, LAT, LON, CH), 1.0, 6.0, ((0, 32), (2, 16))),
        "kernel": centred(key_of[1], (KROWS, CH), KROWS ** -0.5, 0.125),
        "cotangent": centred(key_of[2], (IMAGES, LAT, LON, CH), 1.0, 6.0, ((0, 32), (2, 16))),
        "feedback": centred(key_of[3], (IMAGES, KROWS, CH), 0.5, 4.0, ((0, 32), (1, 16)), jnp.float32),
        "q_start": centred(key_of[4], (CH, RANK), 1.0, 6.0, (), jnp.float32),
    }


def tap_windows(padded, flip_sign, lat_count, lon_count):
    pieces = []
    for lat_step in (-1, 0, 1):
        for lon_step in (-1, 0, 1):
            lat_begin = 1 + flip_sign * lat_step
            lon_begin = 1 + flip_sign * lon_step
            pieces.append(padded[:, lat_begin:lat_begin + lat_count, lon_begin:lon_begin + lon_count, :])
    return jnp.concatenate(pieces, axis=3)

def pad_image(image):
    wrapped = jnp.pad(image, ((0, 0), (0, 0), (1, 1), (0, 0)), mode='wrap')
    return jnp.pad(wrapped, ((0, 0), (1, 1), (0, 0), (0, 0)))

def orthonormal(vectors):
    basis = jnp.zeros_like(vectors)
    for column in range(vectors.shape[1]):
        vector = vectors[:, column]
        projected = jnp.dot(basis.T, vector, precision=lax.Precision.HIGHEST)
        remain = vector - jnp.dot(basis, projected, precision=lax.Precision.HIGHEST)
        sq_norm = jnp.sum(remain * remain)
        basis = basis.at[:, column].set(remain / jnp.sqrt(sq_norm))
    return basis

def reference(inputs, kernel, cotangent, feedback, q_start):
    kernel_rows = 9 * CH
    cells = LAT * LON
    grad_scale = 1.0 / math.sqrt(LAT * LON)
    flipped = kernel.reshape(9, CH, CH).transpose(0, 2, 1).reshape(kernel_rows, CH)

    def per_image(pair):
        image, upstream = pair
        patches = tap_windows(pad_image(image[None]), 1, LAT, LON).reshape(cells, kernel_rows)
        preact = jnp.dot(patches, kernel, preferred_element_type=jnp.float32)
        sigmoid_vals = jax.nn.sigmoid(preact)
        output = (preact * sigmoid_vals).astype(jnp.bfloat16)
        upstream_flat = upstream.reshape(cells, CH).astype(jnp.float32)
        slope = (upstream_flat * sigmoid_vals * (1.0 + preact * (1.0 - sigmoid_vals))).astype(jnp.bfloat16)
        slope_patches = tap_windows(pad_image(slope.reshape(1, LAT, LON, CH)), -1, LAT, LON).reshape(cells, kernel_rows)
        input_grad = jnp.dot(slope_patches, flipped, preferred_element_type=jnp.float32).astype(jnp.bfloat16)
        grad = jnp.dot(patches.T, slope, preferred_element_type=jnp.float32) * grad_scale
        return (output.reshape(LAT, LON, CH), input_grad.reshape(LAT, LON, CH), grad)
    output, input_grad, grad = lax.map(per_image, (inputs, cotangent))
    matrix = grad + feedback
    p_sum = jnp.einsum('irc,ck->rk', matrix, q_start, precision=lax.Precision.HIGHEST) / N_DP
    p_factor = orthonormal(p_sum)
    q_factor = jnp.einsum('irc,rk->ck', matrix, p_factor, precision=lax.Precision.HIGHEST) / N_DP
    approx = jnp.dot(p_factor, q_factor.T, precision=lax.Precision.HIGHEST)
    new_feedback = matrix - approx[None]
    return (output, input_grad, p_factor, q_factor, new_feedback)
```

```python
import functools
import math

import jax
import jax.numpy as jnp
from jax import lax
from jax.experimental import pallas as pl
from jax.experimental.pallas import tpu as pltpu
from jax.sharding import PartitionSpec as P

F32 = jnp.float32
BF16 = jnp.bfloat16
NN = (((1,), (0,)), ((), ()))
NT = (((1,), (1,)), ((), ()))
TN = (((0,), (0,)), ((), ()))
VMEM = pl.BlockSpec(memory_space=pltpu.VMEM)
SMEM = pl.BlockSpec(memory_space=pltpu.SMEM)


def dot(left, right, dims=NN):
    return lax.dot_general(left, right, dims, preferred_element_type=F32)


def in_parts(value):
    parts = []
    for _ in range(3):
        part = value.astype(BF16)
        parts.append(part)
        value = value - part.astype(F32)
    return parts


def stacked_parts(value):
    return jnp.concatenate([part.astype(F32) for part in in_parts(value)], 0).astype(BF16)


def fold(product, rank):
    return product[0:rank] + product[rank : 2 * rank] + product[2 * rank : 3 * rank]


def swish(preact, upstream):
    s = jax.nn.sigmoid(preact)
    return preact * s, upstream * s * (1.0 + preact * (1.0 - s))


def widen(source, left, right, wide, lat, lon, low, high):
    ch = source.shape[1]
    rows = 8 * lon
    column = lax.broadcasted_iota(jnp.int32, (rows, ch), 0) & (lon - 1)
    for step in range(lat // 8):
        value = source[step * rows : (step + 1) * rows, :]
        wider = value.astype(F32)
        edges = [
            jnp.broadcast_to(edge[step * 8 : step * 8 + 8, None, :], (8, lon, ch)).reshape(rows, ch)
            for edge in (left, right)
        ]
        west = jnp.where(column == 0, edges[0], pltpu.roll(wider, 1, 0))
        east = jnp.where(column == lon - 1, edges[1], pltpu.roll(wider, rows - 1, 0))
        at = slice(lon + step * rows, lon + (step + 1) * rows)
        wide[at, low * ch : (low + 1) * ch] = west.astype(BF16)
        wide[at, ch : 2 * ch] = value
        wide[at, high * ch : (high + 1) * ch] = east.astype(BF16)


def conv_kernel(
    lat, lon, tiles, scale, x_ref, cot_ref, w_ref, east_ref, west_ref, left_ref, right_ref, q_ref,
    out_ref, xgrad_ref, wgrad_ref, p_ref, x_wide, s_wide, slope_ref,
):
    cells, ch = x_ref.shape
    rank = q_ref.shape[0]
    chunk = cells // 2
    for wide in (x_wide, s_wide):
        wide[0:lon, :] = jnp.zeros((lon, 3 * ch), BF16)
        wide[lon + cells : 2 * lon + cells, :] = jnp.zeros((lon, 3 * ch), BF16)

    widen(x_ref, left_ref[1].astype(F32), right_ref[0].astype(F32), x_wide, lat, lon, 0, 2)

    def forward(step, carry):
        at = pl.multiple_of(step * chunk, chunk)
        total = dot(x_wide[pl.ds(at, chunk), :], w_ref[0 : 3 * ch, :])
        total += dot(x_wide[pl.ds(at + lon, chunk), :], w_ref[3 * ch : 6 * ch, :])
        total += dot(x_wide[pl.ds(at + 2 * lon, chunk), :], w_ref[6 * ch : 9 * ch, :])
        out, slope = swish(total, cot_ref[pl.ds(at, chunk), :].astype(F32))
        out_ref[pl.ds(at, chunk), :] = out.astype(BF16)
        slope_ref[pl.ds(at, chunk), :] = slope.astype(BF16)
        return carry

    lax.fori_loop(0, cells // chunk, forward, 0)

    columns = [
        jnp.concatenate([west.astype(F32), east.astype(F32)], 0)
        for west, east in (
            (left_ref[0], east_ref[1]),
            (left_ref[1], right_ref[0]),
            (west_ref[0], right_ref[1]),
        )
    ]
    row = lax.broadcasted_iota(jnp.int32, (2 * lat, ch), 0) & (lat - 1)
    total = jnp.zeros((2 * lat, ch), F32)
    for a in range(3):
        for b in range(3):
            value = columns[b]
            if a == 0:
                value = jnp.where(row == 0, 0.0, pltpu.roll(value, 1, 0))
            if a == 2:
                value = jnp.where(row == lat - 1, 0.0, pltpu.roll(value, 2 * lat - 1, 0))
            tap = 3 * a + b
            total += dot(value.astype(BF16), w_ref[tap * ch : (tap + 1) * ch, :])
    upstream = jnp.concatenate([left_ref[2].astype(F32), right_ref[2].astype(F32)], 0)
    edge = swish(total, upstream)[1].astype(BF16).astype(F32)
    widen(slope_ref, edge[:lat], edge[lat:], s_wide, lat, lon, 2, 0)

    def input_grad(step, carry):
        at = pl.multiple_of(step * chunk, chunk)
        total = None
        for a in range(3):
            for b in range(3):
                tap = 3 * a + b
                term = dot(
                    s_wide[pl.ds(at + (2 - a) * lon, chunk), b * ch : (b + 1) * ch],
                    w_ref[tap * ch : (tap + 1) * ch, :],
                    NT,
                )
                total = term if total is None else total + term
        xgrad_ref[pl.ds(at, chunk), :] = total.astype(BF16)
        return carry

    lax.fori_loop(0, cells // chunk, input_grad, 0)

    def weight_grad(a, carry):
        at = pl.multiple_of(a * lon, lon)
        for b in range(3):
            term = dot(x_wide[pl.ds(at, cells), b * ch : (b + 1) * ch], slope_ref[...], TN) * scale
            wgrad_ref[pl.ds(pl.multiple_of((3 * a + b) * ch, ch), ch), :] = term.astype(BF16)
        return carry

    lax.fori_loop(0, 3, weight_grad, 0)

    q_parts = stacked_parts(q_ref[...])
    rows = wgrad_ref.shape[0] // tiles
    for t in range(tiles):
        p_ref[t] = fold(dot(q_parts, wgrad_ref[rows * t : rows * (t + 1), :], NT), rank)


def factor_kernel(tiles, tile_ref, p_ref, wgrad_ref, error_ref, rows_ref, q_ref, flat, cut):
    rank, rows = p_ref.shape[1:]
    for t in range(tiles):
        flat[:, rows * t : rows * (t + 1)] = p_ref[t]
    vectors = flat[...]
    lane = lax.broadcasted_iota(jnp.int32, vectors.shape, 0)
    basis = jnp.zeros_like(vectors)
    for column in range(rank):
        vector = vectors[column : column + 1, :]
        remain = vector
        if column:
            projected = jnp.sum(basis * vector, axis=1, keepdims=True)
            remain = vector - jnp.sum(basis * projected, axis=0, keepdims=True)
        sq_norm = jnp.sum(remain * remain, axis=1, keepdims=True)
        basis = jnp.where(lane == column, remain / jnp.sqrt(sq_norm), basis)
    for t in range(tiles):
        cut[t] = basis[:, rows * t : rows * (t + 1)]
    own = cut[tile_ref[0]]
    rows_ref[...] = own
    total = fold(dot(stacked_parts(basis), wgrad_ref[...]), rank)
    own_parts = stacked_parts(own)
    for part in in_parts(error_ref[...]):
        total += fold(dot(own_parts, part), rank)
    q_ref[...] = total


def feedback_kernel(shares, matrix_ref, error_ref, rows_ref, q_ref, next_ref, factor_ref, left_ref):
    rank = rows_ref.shape[0]
    q_mean = q_ref[0]
    for image in range(1, shares):
        q_mean += q_ref[image]
    q_mean = q_mean * (1.0 / shares)
    factor_ref[...] = q_mean.T
    own = rows_ref[...].T
    left_ref[...] = own
    total = matrix_ref[...].astype(F32) + error_ref[...]
    for k in range(rank):
        total -= own[:, k : k + 1] * q_mean[k : k + 1, :]
    next_ref[...] = total


def shift(axis, step):
    count = lax.axis_size(axis)
    return [(i, (i + step) % count) for i in range(count)]


def shares_of(value, axis):
    count = lax.axis_size(axis)
    return lax.all_to_all(
        jnp.broadcast_to(value[None], (count,) + value.shape), axis, 0, 0, tiled=True
    )


def per_device(inputs, kernel, cotangent, feedback, q_start):
    _, lat, lon, ch = inputs.shape
    kernel_rows = kernel.shape[0]
    rows_dev = feedback.shape[1]
    rank = q_start.shape[1]
    cells = lat * lon
    tiles = lax.axis_size("tile")
    images = lax.axis_size("dp")
    scale = 1.0 / math.sqrt(cells * tiles)
    x, upstream, error = inputs[0], cotangent[0], feedback[0]

    def edge(*columns):
        return jnp.stack(columns)

    east = edge(x[:, lon - 2], x[:, lon - 1], upstream[:, lon - 1])
    west = edge(x[:, 0], x[:, 1], upstream[:, 0])
    left = lax.ppermute(east, "tile", shift("tile", 1))
    right = lax.ppermute(west, "tile", shift("tile", -1))

    q_rows = q_start.T
    sds = jax.ShapeDtypeStruct
    out, xgrad, wgrad, p_shares = pl.pallas_call(
        functools.partial(conv_kernel, lat, lon, tiles, scale),
        out_shape=(
            sds((cells, ch), BF16),
            sds((cells, ch), BF16),
            sds((kernel_rows, ch), BF16),
            sds((tiles, rank, rows_dev), F32),
        ),
        in_specs=[VMEM] * 8,
        out_specs=(VMEM,) * 4,
        scratch_shapes=[
            pltpu.VMEM((cells + 2 * lon, 3 * ch), BF16),
            pltpu.VMEM((cells + 2 * lon, 3 * ch), BF16),
            pltpu.VMEM((cells, ch), BF16),
        ],
        compiler_params=pltpu.CompilerParams(vmem_limit_bytes=40 * 2**20),
        name="conv",
    )(x.reshape(cells, ch), upstream.reshape(cells, ch), kernel, east, west, left, right, q_rows)

    matrix = lax.psum_scatter(wgrad, "tile", scatter_dimension=0, tiled=True)

    error_rows = lax.dot_general(q_rows, error, NT, precision=lax.Precision.HIGHEST)
    p_local = lax.all_to_all(p_shares, "tile", 0, 0, tiled=True).sum(0) + error_rows
    p_rows = shares_of(p_local, "dp").sum(0) * (1.0 / images)
    p_all = shares_of(p_rows, "tile")

    tile = lax.axis_index("tile").astype(jnp.int32)[None]
    own_rows, q_part = pl.pallas_call(
        functools.partial(factor_kernel, tiles),
        out_shape=(sds((rank, rows_dev), F32), sds((rank, ch), F32)),
        in_specs=[SMEM] + [VMEM] * 3,
        out_specs=(VMEM,) * 2,
        scratch_shapes=[
            pltpu.VMEM((rank, kernel_rows), F32),
            pltpu.VMEM((tiles, rank, rows_dev), F32),
        ],
        compiler_params=pltpu.CompilerParams(vmem_limit_bytes=16 * 2**20),
        name="factor",
    )(tile, p_all, wgrad, error)

    q_shares = shares_of(shares_of(q_part, "tile").sum(0), "dp")
    new_feedback, q_factor, p_factor = pl.pallas_call(
        functools.partial(feedback_kernel, images),
        out_shape=(sds((rows_dev, ch), F32), sds((ch, rank), F32), sds((rows_dev, rank), F32)),
        in_specs=[VMEM] * 4,
        out_specs=(VMEM,) * 3,
        compiler_params=pltpu.CompilerParams(vmem_limit_bytes=16 * 2**20),
        name="residual",
    )(matrix, error, own_rows, q_shares)

    shape = inputs.shape
    return (out.reshape(shape), xgrad.reshape(shape), p_factor, q_factor, new_feedback[None])


def solution(mesh):
    in_specs = (
        P("dp", None, "tile", None),
        P(),
        P("dp", None, "tile", None),
        P("dp", "tile", None),
        P(),
    )
    out_specs = (
        P("dp", None, "tile", None),
        P("dp", None, "tile", None),
        P("tile", None),
        P(),
        P("dp", "tile", None),
    )
    return jax.shard_map(
        per_device, mesh=mesh, in_specs=in_specs, out_specs=out_specs, check_vma=False
    )
```

```python
import functools
import math

import jax
import jax.numpy as jnp
from jax import lax
from jax.experimental import pallas as pl
from jax.experimental.pallas import tpu as pltpu
from jax.sharding import PartitionSpec as P

F32 = jnp.float32
BF16 = jnp.bfloat16
NN = (((1,), (0,)), ((), ()))
NT = (((1,), (1,)), ((), ()))
TN = (((0,), (0,)), ((), ()))
VMEM = pl.BlockSpec(memory_space=pltpu.VMEM)
HBM = pl.BlockSpec(memory_space=pl.ANY)
BIG = 24 * 2**20
WHOLE = 56 * 2**20


def dot(left, right, dims=NN):
    return lax.dot_general(left, right, dims, preferred_element_type=F32)


def in_parts(value):
    parts = []
    for _ in range(3):
        part = value.astype(BF16)
        parts.append(part)
        value = value - part.astype(F32)
    return parts


def stacked_parts(value):
    return jnp.concatenate([part.astype(F32) for part in in_parts(value)], 0).astype(BF16)


def fold(product, rank):
    return product[0:rank] + product[rank : 2 * rank] + product[2 * rank : 3 * rank]


def fetch(pairs, sems):
    copies = [pltpu.make_async_copy(held, place, sems.at[k]) for k, (held, place) in enumerate(pairs)]
    for copy in copies:
        copy.start()
    return copies


def swish(preact, upstream):
    s = jax.nn.sigmoid(preact)
    return preact * s, upstream * s * (1.0 + preact * (1.0 - s))


def widen(source, left, right, wide, lat, lon, low, high):
    ch = source.shape[1]
    rows = 8 * lon
    column = lax.broadcasted_iota(jnp.int32, (rows, ch), 0) & (lon - 1)
    wide[0:lon, :] = jnp.zeros((lon, 3 * ch), BF16)
    wide[lon + lat * lon :, :] = jnp.zeros((lon, 3 * ch), BF16)
    for step in range(lat // 8):
        value = source[step * rows : (step + 1) * rows, :]
        wider = value.astype(F32)
        edges = [spread(edge, step, lon) for edge in (left, right)]
        west = jnp.where(column == 0, edges[0], pltpu.roll(wider, 1, 0))
        east = jnp.where(column == lon - 1, edges[1], pltpu.roll(wider, rows - 1, 0))
        at = slice(lon + step * rows, lon + (step + 1) * rows)
        wide[at, low * ch : (low + 1) * ch] = west.astype(BF16)
        wide[at, ch : 2 * ch] = value
        wide[at, high * ch : (high + 1) * ch] = east.astype(BF16)


def spread(edge, step, lon):
    if edge is None:
        return 0.0
    ch = edge.shape[1]
    part = edge[step * 8 : step * 8 + 8, None, :]
    return jnp.broadcast_to(part, (8, lon, ch)).reshape(8 * lon, ch)


def picked(columns, source, lat, lon):
    shape = (lat * len(columns), lat * lon)
    cell = lax.broadcasted_iota(jnp.int32, shape, 1)
    row = lax.broadcasted_iota(jnp.int32, shape, 0)
    target = (row & (lat - 1)) * lon
    for k, column in enumerate(columns):
        target = jnp.where((row >= k * lat) & (row < (k + 1) * lat), target + column, target)
    return dot((cell == target).astype(F32).astype(BF16), source[...]).astype(BF16)


def load_kernel(
    lat, lon, x_hbm, cot_hbm, w_hbm, x_ref, cot_ref, w_ref, east_ref, west_ref, sems
):
    x_copy, cot_copy, w_copy = fetch([(x_hbm, x_ref), (cot_hbm, cot_ref), (w_hbm, w_ref)], sems)
    x_copy.wait()
    x_edge = picked((0, 1, lon - 2, lon - 1), x_ref, lat, lon)
    west_ref[0] = x_edge[0:lat]
    west_ref[1] = x_edge[lat : 2 * lat]
    east_ref[0] = x_edge[2 * lat : 3 * lat]
    east_ref[1] = x_edge[3 * lat : 4 * lat]
    cot_copy.wait()
    cot_edge = picked((0, lon - 1), cot_ref, lat, lon)
    west_ref[2] = cot_edge[0:lat]
    east_ref[2] = cot_edge[lat : 2 * lat]
    w_copy.wait()


def inner_kernel(lat, lon, x_ref, w_ref, x_wide, preact_ref):
    cells, ch = x_ref.shape
    chunk = cells // 2
    widen(x_ref, None, None, x_wide, lat, lon, 0, 2)

    def forward(step, carry):
        at = pl.multiple_of(step * chunk, chunk)
        total = dot(x_wide[pl.ds(at, chunk), :], w_ref[0 : 3 * ch, :])
        total += dot(x_wide[pl.ds(at + lon, chunk), :], w_ref[3 * ch : 6 * ch, :])
        total += dot(x_wide[pl.ds(at + 2 * lon, chunk), :], w_ref[6 * ch : 9 * ch, :])
        preact_ref[pl.ds(at, chunk), :] = total
        return carry

    lax.fori_loop(0, cells // chunk, forward, 0)


def conv_kernel(
    lat, lon, scale, x_wide, preact_ref, cot_ref, w_ref, east_ref, west_ref, left_ref, right_ref,
    out_hbm, slope_ref, edge_ref, keep_ref, send_ref, out_ref, wgrad_ref, out_sem,
):
    cells, ch = cot_ref.shape
    core = lax.axis_index("tile") & 1
    tap = lambda k: w_ref[k * ch : (k + 1) * ch, :]

    columns = [
        jnp.concatenate([west.astype(F32), east.astype(F32)], 0)
        for west, east in (
            (left_ref[0], east_ref[1]),
            (left_ref[1], right_ref[0]),
            (west_ref[0], right_ref[1]),
        )
    ]
    row = lax.broadcasted_iota(jnp.int32, (2 * lat, ch), 0) & (lat - 1)

    def at_latitude(value, a):
        if a == 0:
            value = jnp.where(row == 0, 0.0, pltpu.roll(value, 1, 0))
        if a == 2:
            value = jnp.where(row == lat - 1, 0.0, pltpu.roll(value, 2 * lat - 1, 0))
        return value.astype(BF16)

    columns = [[at_latitude(value, a) for a in range(3)] for value in columns]

    west = sum(dot(columns[1][a][0:lat], tap(3 * a)) for a in range(3))
    east = sum(dot(columns[1][a][lat : 2 * lat], tap(3 * a + 2)) for a in range(3))
    rows = 8 * lon
    column = lax.broadcasted_iota(jnp.int32, (rows, ch), 0) & (lon - 1)
    for step in range(lat // 8):
        at = slice(step * rows, (step + 1) * rows)
        preact = preact_ref[at, :]
        preact += jnp.where(column == 0, spread(west, step, lon), 0.0)
        preact += jnp.where(column == lon - 1, spread(east, step, lon), 0.0)
        out, slope = swish(preact, cot_ref[at, :].astype(F32))
        out_ref[at, :] = out.astype(BF16)
        slope_ref[at, :] = slope.astype(BF16)
    out_copy = pltpu.make_async_copy(out_ref, out_hbm, out_sem)
    out_copy.start()

    total = jnp.zeros((2 * lat, ch), F32)
    for a in range(3):
        for b in range(3):
            total += dot(columns[b][a], tap(3 * a + b))
    upstream = jnp.concatenate([left_ref[2].astype(F32), right_ref[2].astype(F32)], 0)
    edge_ref[...] = swish(total, upstream)[1].astype(BF16)

    own_edge = picked((0, lon - 1), slope_ref, lat, lon)
    for k in range(9):
        a, b = k // 3, k % 3
        term = dot(x_wide[a * lon : a * lon + cells, b * ch : (b + 1) * ch], slope_ref[...], TN)
        if b == 0:
            term += dot(columns[1][a][0:lat], own_edge[0:lat], TN)
        if b == 2:
            term += dot(columns[1][a][lat : 2 * lat], own_edge[lat : 2 * lat], TN)
        wgrad_ref[k * ch : (k + 1) * ch, :] = (term * scale).astype(BF16)
    pairs, piece, _ = keep_ref.shape
    for pair in range(pairs):
        for held, owner in ((keep_ref, core), (send_ref, 1 - core)):
            start = pl.multiple_of((2 * pair + owner) * piece, 16)
            held[pair] = wgrad_ref[pl.ds(start, piece), :]
    out_copy.wait()


def conv_call(x, upstream, kernel, lat, lon, tiles, rows_dev, scale):
    cells, ch = x.shape
    kernel_rows = kernel.shape[0]
    sds, local = jax.ShapeDtypeStruct, pltpu.VMEM
    image = local((cells, ch), BF16)
    edges = local((3, lat, ch), BF16)
    x, upstream, kernel, east, west = pl.pallas_call(
        functools.partial(load_kernel, lat, lon),
        out_shape=(image, image, local((kernel_rows, ch), BF16), edges, edges),
        in_specs=[HBM] * 3,
        out_specs=(VMEM,) * 5,
        scratch_shapes=[pltpu.SemaphoreType.DMA((3,))],
        compiler_params=pltpu.CompilerParams(vmem_limit_bytes=WHOLE),
        name="load",
    )(x, upstream, kernel)
    left = lax.ppermute(east, "tile", shift("tile", 1))
    right = lax.ppermute(west, "tile", shift("tile", -1))
    wide, preact = pl.pallas_call(
        functools.partial(inner_kernel, lat, lon),
        out_shape=(local((cells + 2 * lon, 3 * ch), BF16), local((cells, ch), F32)),
        in_specs=[VMEM] * 2,
        out_specs=(VMEM,) * 2,
        compiler_params=pltpu.CompilerParams(vmem_limit_bytes=BIG),
        cost_estimate=pl.CostEstimate(
            flops=2 * cells * kernel_rows * ch, bytes_accessed=0, transcendentals=0
        ),
        name="inner",
    )(x, kernel)
    half = local((tiles // 2, rows_dev, ch), BF16)
    out, slope, edge, keep, send = pl.pallas_call(
        functools.partial(conv_kernel, lat, lon, scale),
        out_shape=(sds((cells, ch), BF16), image, local((2 * lat, ch), BF16), half, half),
        in_specs=[VMEM] * 8,
        out_specs=(HBM,) + (VMEM,) * 4,
        scratch_shapes=[
            pltpu.VMEM((cells, ch), BF16),
            pltpu.VMEM((kernel_rows, ch), BF16),
            pltpu.SemaphoreType.DMA,
        ],
        compiler_params=pltpu.CompilerParams(vmem_limit_bytes=BIG),
        cost_estimate=pl.CostEstimate(
            flops=2 * cells * kernel_rows * ch, bytes_accessed=2**20, transcendentals=cells * ch
        ),
        name="conv",
    )(wide, preact, upstream, kernel, east, west, left, right)
    return out, slope, edge, keep, send, kernel


def input_grad_kernel(lat, lon, slope_ref, edge_ref, w_ref, xgrad_ref, s_wide):
    cells, ch = slope_ref.shape
    chunk = cells // 2
    edge = edge_ref[...].astype(F32)
    widen(slope_ref, edge[:lat], edge[lat:], s_wide, lat, lon, 2, 0)

    def input_grad(step, carry):
        at = pl.multiple_of(step * chunk, chunk)
        total = None
        for a in range(3):
            for b in range(3):
                tap = 3 * a + b
                term = dot(
                    s_wide[pl.ds(at + (2 - a) * lon, chunk), b * ch : (b + 1) * ch],
                    w_ref[tap * ch : (tap + 1) * ch, :],
                    NT,
                )
                total = term if total is None else total + term
        xgrad_ref[pl.ds(at, chunk), :] = total.astype(BF16)
        return carry

    lax.fori_loop(0, cells // chunk, input_grad, 0)


def matrix_kernel(wgrad_ref, error_ref, q_ref, matrix_ref, p_ref):
    matrix = wgrad_ref[0].astype(F32)
    for t in range(1, wgrad_ref.shape[0]):
        matrix += wgrad_ref[t].astype(F32)
    matrix += error_ref[...]
    matrix_ref[...] = matrix
    q_parts = stacked_parts(q_ref[...])
    p_rows = jnp.zeros(p_ref.shape, F32)
    for part in in_parts(matrix):
        p_rows += fold(dot(q_parts, part, NT), q_ref.shape[0])
    p_ref[...] = p_rows


def moment_kernel(matrix_ref, p_ref, rows_ref, moment_ref):
    images, rank, rows = p_ref.shape
    ch = matrix_ref.shape[1]
    p_rows = p_ref[0]
    for image in range(1, images):
        p_rows += p_ref[image]
    p_rows = p_rows * (1.0 / images)
    rows_ref[...] = p_rows
    p_parts = stacked_parts(p_rows)
    moment = jnp.zeros((rank, ch), F32)
    for part in in_parts(matrix_ref[...]):
        moment += fold(dot(p_parts, part), rank)
    moment_ref[:, 0:ch] = moment
    gram = jnp.zeros((rank, 128), F32)
    for part in in_parts(p_rows):
        padded = jnp.concatenate([part.astype(F32), jnp.zeros((128 - rank, rows), F32)], 0)
        gram += fold(dot(p_parts, padded.astype(BF16), NT), rank)
    moment_ref[:, ch : ch + 128] = gram


def factor_kernel(gram_ref, p_ref, left_ref, held_ref, solve_ref):
    rank = p_ref.shape[0]
    gram = gram_ref[...]
    p_rows = p_ref[...]
    index = lax.broadcasted_iota(jnp.int32, (rank, 1), 0)
    lane = lax.broadcasted_iota(jnp.int32, (rank, 128), 1)
    solve = jnp.where(lane == index, 1.0, 0.0)
    for j in range(rank):
        floor = 1e-14 * gram_ref[j : j + 1, j : j + 1]
        inverse = 1.0 / jnp.sqrt(jnp.maximum(gram[j : j + 1, j : j + 1], floor))
        projected = jnp.where(index > j, gram[:, j : j + 1] * inverse, 0.0)

        def step(value):
            unit = value[j : j + 1, :] * inverse
            return jnp.where(index == j, unit, value - projected * unit)

        gram, p_rows, solve = step(gram), step(p_rows), step(solve)
    left_ref[...] = p_rows
    held_ref[...] = p_rows
    solve_ref[...] = solve


def residual_kernel(matrix_ref, left_ref, solve_ref, s_ref, next_ref, right_ref):
    images, rank, _ = s_ref.shape
    mean = s_ref[0]
    for image in range(1, images):
        mean += s_ref[image]
    mean = mean * (1.0 / images)
    solve = solve_ref[...]
    right = solve[:, 0:1] * mean[0:1, :]
    for k in range(1, rank):
        right += solve[:, k : k + 1] * mean[k : k + 1, :]
    right_ref[...] = right
    columns = left_ref[...].T
    total = matrix_ref[...]
    for k in range(rank):
        total -= columns[:, k : k + 1] * right[k : k + 1, :]
    next_ref[...] = total


def shift(axis, step):
    count = lax.axis_size(axis)
    return [(i, (i + step) % count) for i in range(count)]


def cores(axis):
    return [(i, i ^ 1) for i in range(lax.axis_size(axis))]


def chips(axis):
    count = lax.axis_size(axis)
    return [list(range(core, count, 2)) for core in range(2)]


def shares_of(value, axis):
    count = lax.axis_size(axis)
    return lax.all_to_all(
        jnp.broadcast_to(value[None], (count,) + value.shape), axis, 0, 0, tiled=True
    )


def per_device(inputs, kernel, cotangent, feedback, q_start):
    _, lat, lon, ch = inputs.shape
    kernel_rows = kernel.shape[0]
    rows_dev = feedback.shape[1]
    rank = q_start.shape[1]
    cells = lat * lon
    tiles = lax.axis_size("tile")
    scale = 1.0 / math.sqrt(cells * tiles)
    x, upstream, error = inputs[0], cotangent[0], feedback[0]

    x_cells, upstream_cells = x.reshape(cells, ch), upstream.reshape(cells, ch)
    sds, local = jax.ShapeDtypeStruct, pltpu.VMEM
    out, slope, edge, keep, send, held_kernel = conv_call(
        x_cells, upstream_cells, kernel, lat, lon, tiles, rows_dev, scale
    )
    xgrad = pl.pallas_call(
        functools.partial(input_grad_kernel, lat, lon),
        out_shape=sds((cells, ch), BF16),
        in_specs=[VMEM] * 3,
        out_specs=VMEM,
        scratch_shapes=[pltpu.VMEM((cells + 2 * lon, 3 * ch), BF16)],
        compiler_params=pltpu.CompilerParams(vmem_limit_bytes=BIG),
        cost_estimate=pl.CostEstimate(
            flops=2 * cells * kernel_rows * ch, bytes_accessed=2 * 2**20, transcendentals=0
        ),
        name="input_grad",
    )(slope, edge, held_kernel)

    summed = keep + lax.ppermute(send, "tile", cores("tile"))
    wgrad_rows = lax.all_to_all(
        summed, "tile", 0, 0, axis_index_groups=chips("tile"), tiled=True
    )
    small = pltpu.CompilerParams(vmem_limit_bytes=16 * 2**20)
    matrix, p_local = pl.pallas_call(
        matrix_kernel,
        out_shape=(local((rows_dev, ch), F32), local((rank, rows_dev), F32)),
        in_specs=[VMEM] * 3,
        out_specs=(VMEM,) * 2,
        compiler_params=small,
        name="matrix",
    )(wgrad_rows, error, q_start.T)
    p_rows, moment = pl.pallas_call(
        moment_kernel,
        out_shape=(sds((rank, rows_dev), F32), sds((rank, ch + 128), F32)),
        in_specs=[VMEM] * 2,
        out_specs=(VMEM,) * 2,
        compiler_params=small,
        name="moment",
    )(matrix, shares_of(p_local, "dp"))
    moment = shares_of(moment, "tile").sum(0)
    p_factor, held_factor, solve = pl.pallas_call(
        factor_kernel,
        out_shape=(
            sds((rank, rows_dev), F32),
            local((rank, rows_dev), F32),
            local((rank, 128), F32),
        ),
        in_specs=[VMEM] * 2,
        out_specs=(VMEM,) * 3,
        compiler_params=small,
        name="factor",
    )(moment[:, ch:], p_rows)
    new_feedback, q_factor = pl.pallas_call(
        residual_kernel,
        out_shape=(sds((rows_dev, ch), F32), sds((rank, ch), F32)),
        in_specs=[VMEM] * 4,
        out_specs=(VMEM,) * 2,
        compiler_params=small,
        name="residual",
    )(matrix, held_factor, solve, shares_of(moment[:, :ch], "dp"))

    shape = inputs.shape
    return (out.reshape(shape), xgrad.reshape(shape), p_factor.T, q_factor.T, new_feedback[None])


def solution(mesh):
    in_specs = (
        P("dp", None, "tile", None),
        P(),
        P("dp", None, "tile", None),
        P("dp", "tile", None),
        P(),
    )
    out_specs = (
        P("dp", None, "tile", None),
        P("dp", None, "tile", None),
        P("tile", None),
        P(),
        P("dp", "tile", None),
    )
    return jax.shard_map(
        per_device, mesh=mesh, in_specs=in_specs, out_specs=out_specs, check_vma=False
    )
```

```python
import functools
import math

import jax
import jax.numpy as jnp
from jax import lax
from jax.experimental import pallas as pl
from jax.experimental.pallas import tpu as pltpu
from jax.sharding import PartitionSpec as P

F32 = jnp.float32
BF16 = jnp.bfloat16
NN = (((1,), (0,)), ((), ()))
NT = (((1,), (1,)), ((), ()))
TN = (((0,), (0,)), ((), ()))
VMEM = pl.BlockSpec(memory_space=pltpu.VMEM)
HBM = pl.BlockSpec(memory_space=pl.ANY)
BIG = 24 * 2**20
WHOLE = 56 * 2**20


def dot(left, right, dims=NN):
    return lax.dot_general(left, right, dims, preferred_element_type=F32)


def in_parts(value):
    parts = []
    for _ in range(3):
        part = value.astype(BF16)
        parts.append(part)
        value = value - part.astype(F32)
    return parts


def stacked_parts(value):
    return jnp.concatenate([part.astype(F32) for part in in_parts(value)], 0).astype(BF16)


def fold(product, rank):
    return product[0:rank] + product[rank : 2 * rank] + product[2 * rank : 3 * rank]


def fetch(pairs, sems):
    copies = [pltpu.make_async_copy(held, place, sems.at[k]) for k, (held, place) in enumerate(pairs)]
    for copy in copies:
        copy.start()
    return copies


def swish(preact, upstream):
    s = jax.nn.sigmoid(preact)
    return preact * s, upstream * s * (1.0 + preact * (1.0 - s))


def widen(source, left, right, wide, lat, lon, low, high):
    ch = source.shape[1]
    rows = 8 * lon
    column = lax.broadcasted_iota(jnp.int32, (rows, ch), 0) & (lon - 1)
    wide[0:lon, :] = jnp.zeros((lon, 3 * ch), BF16)
    wide[lon + lat * lon :, :] = jnp.zeros((lon, 3 * ch), BF16)
    for step in range(lat // 8):
        value = source[step * rows : (step + 1) * rows, :]
        wider = value.astype(F32)
        edges = [spread(edge, step, lon) for edge in (left, right)]
        west = jnp.where(column == 0, edges[0], pltpu.roll(wider, 1, 0))
        east = jnp.where(column == lon - 1, edges[1], pltpu.roll(wider, rows - 1, 0))
        at = slice(lon + step * rows, lon + (step + 1) * rows)
        wide[at, low * ch : (low + 1) * ch] = west.astype(BF16)
        wide[at, ch : 2 * ch] = value
        wide[at, high * ch : (high + 1) * ch] = east.astype(BF16)


def spread(edge, step, lon):
    if edge is None:
        return 0.0
    ch = edge.shape[1]
    part = edge[step * 8 : step * 8 + 8, None, :]
    return jnp.broadcast_to(part, (8, lon, ch)).reshape(8 * lon, ch)


def picked(columns, source, lat, lon):
    shape = (lat * len(columns), lat * lon)
    cell = lax.broadcasted_iota(jnp.int32, shape, 1)
    row = lax.broadcasted_iota(jnp.int32, shape, 0)
    target = (row & (lat - 1)) * lon
    for k, column in enumerate(columns):
        target = jnp.where((row >= k * lat) & (row < (k + 1) * lat), target + column, target)
    return dot((cell == target).astype(F32).astype(BF16), source[...]).astype(BF16)


def load_kernel(
    lat, lon, x_hbm, cot_hbm, w_hbm, x_ref, cot_ref, w_ref, east_ref, west_ref, sems
):
    x_copy, cot_copy, w_copy = fetch([(x_hbm, x_ref), (cot_hbm, cot_ref), (w_hbm, w_ref)], sems)
    x_copy.wait()
    x_edge = picked((0, 1, lon - 2, lon - 1), x_ref, lat, lon)
    west_ref[0] = x_edge[0:lat]
    west_ref[1] = x_edge[lat : 2 * lat]
    east_ref[0] = x_edge[2 * lat : 3 * lat]
    east_ref[1] = x_edge[3 * lat : 4 * lat]
    cot_copy.wait()
    cot_edge = picked((0, lon - 1), cot_ref, lat, lon)
    west_ref[2] = cot_edge[0:lat]
    east_ref[2] = cot_edge[lat : 2 * lat]
    w_copy.wait()


def inner_kernel(lat, lon, x_ref, w_ref, x_wide, preact_ref):
    cells, ch = x_ref.shape
    chunk = cells // 2
    widen(x_ref, None, None, x_wide, lat, lon, 0, 2)

    def forward(step, carry):
        at = pl.multiple_of(step * chunk, chunk)
        total = dot(x_wide[pl.ds(at, chunk), :], w_ref[0 : 3 * ch, :])
        total += dot(x_wide[pl.ds(at + lon, chunk), :], w_ref[3 * ch : 6 * ch, :])
        total += dot(x_wide[pl.ds(at + 2 * lon, chunk), :], w_ref[6 * ch : 9 * ch, :])
        preact_ref[pl.ds(at, chunk), :] = total
        return carry

    lax.fori_loop(0, cells // chunk, forward, 0)


def shifted(west, east, lat):
    value = jnp.concatenate([west.astype(F32), east.astype(F32)], 0)
    row = lax.broadcasted_iota(jnp.int32, value.shape, 0) & (lat - 1)
    south = jnp.where(row == 0, 0.0, pltpu.roll(value, 1, 0))
    north = jnp.where(row == lat - 1, 0.0, pltpu.roll(value, 2 * lat - 1, 0))
    return [south.astype(BF16), value.astype(BF16), north.astype(BF16)]


def conv_kernel(
    lat, lon, scale, x_wide, preact_ref, cot_ref, w_ref, left_ref, right_ref,
    out_ref, slope_ref, keep_ref, send_ref, x_sides, wgrad_ref,
):
    cells, ch = cot_ref.shape
    core = lax.axis_index("tile") & 1
    tap = lambda k: w_ref[k * ch : (k + 1) * ch, :]

    beside = shifted(left_ref[1], right_ref[0], lat)

    west = sum(dot(beside[a][0:lat], tap(3 * a)) for a in range(3))
    east = sum(dot(beside[a][lat : 2 * lat], tap(3 * a + 2)) for a in range(3))
    rows = 8 * lon
    column = lax.broadcasted_iota(jnp.int32, (rows, ch), 0) & (lon - 1)
    for step in range(lat // 8):
        at = slice(step * rows, (step + 1) * rows)
        preact = preact_ref[at, :]
        preact += jnp.where(column == 0, spread(west, step, lon), 0.0)
        preact += jnp.where(column == lon - 1, spread(east, step, lon), 0.0)
        out, slope = swish(preact, cot_ref[at, :].astype(F32))
        out_ref[at, :] = out.astype(BF16)
        slope_ref[at, :] = slope.astype(BF16)
        wide_at = slice(lon + step * rows, lon + (step + 1) * rows)
        for side, place, edge in ((0, 0, left_ref[1]), (1, lon - 1, right_ref[0])):
            value = x_wide[wide_at, 2 * side * ch : (2 * side + 1) * ch].astype(F32)
            value = jnp.where(column == place, spread(edge.astype(F32), step, lon), value)
            x_sides[wide_at, side * ch : (side + 1) * ch] = value.astype(BF16)
    x_sides[0:lon, :] = jnp.zeros((lon, 2 * ch), BF16)
    x_sides[lon + cells :, :] = jnp.zeros((lon, 2 * ch), BF16)

    for k in range(9):
        a, b = k // 3, k % 3
        source, block = (x_wide, 1) if b == 1 else (x_sides, b // 2)
        term = dot(
            source[a * lon : a * lon + cells, block * ch : (block + 1) * ch], slope_ref[...], TN
        )
        wgrad_ref[k * ch : (k + 1) * ch, :] = (term * scale).astype(BF16)
    pairs, piece, _ = keep_ref.shape
    for pair in range(pairs):
        for held, owner in ((keep_ref, core), (send_ref, 1 - core)):
            start = pl.multiple_of((2 * pair + owner) * piece, 16)
            held[pair] = wgrad_ref[pl.ds(start, piece), :]


def conv_call(x, upstream, kernel, lat, lon, tiles, rows_dev, scale):
    cells, ch = x.shape
    kernel_rows = kernel.shape[0]
    sds, local = jax.ShapeDtypeStruct, pltpu.VMEM
    image = local((cells, ch), BF16)
    edges = local((3, lat, ch), BF16)
    x, upstream, kernel, east, west = pl.pallas_call(
        functools.partial(load_kernel, lat, lon),
        out_shape=(image, image, local((kernel_rows, ch), BF16), edges, edges),
        in_specs=[HBM] * 3,
        out_specs=(VMEM,) * 5,
        scratch_shapes=[pltpu.SemaphoreType.DMA((3,))],
        compiler_params=pltpu.CompilerParams(vmem_limit_bytes=WHOLE),
        name="load",
    )(x, upstream, kernel)
    left = lax.ppermute(east, "tile", shift("tile", 1))
    right = lax.ppermute(west, "tile", shift("tile", -1))
    wide, preact = pl.pallas_call(
        functools.partial(inner_kernel, lat, lon),
        out_shape=(local((cells + 2 * lon, 3 * ch), BF16), local((cells, ch), F32)),
        in_specs=[VMEM] * 2,
        out_specs=(VMEM,) * 2,
        compiler_params=pltpu.CompilerParams(vmem_limit_bytes=BIG),
        cost_estimate=pl.CostEstimate(
            flops=2 * cells * kernel_rows * ch, bytes_accessed=0, transcendentals=0
        ),
        name="inner",
    )(x, kernel)
    half = local((tiles // 2, rows_dev, ch), BF16)
    out, slope, keep, send = pl.pallas_call(
        functools.partial(conv_kernel, lat, lon, scale),
        out_shape=(image, image, half, half),
        in_specs=[VMEM] * 6,
        out_specs=(VMEM,) * 4,
        scratch_shapes=[
            pltpu.VMEM((cells + 2 * lon, 2 * ch), BF16),
            pltpu.VMEM((kernel_rows, ch), BF16),
        ],
        compiler_params=pltpu.CompilerParams(vmem_limit_bytes=BIG),
        cost_estimate=pl.CostEstimate(
            flops=2 * cells * kernel_rows * ch, bytes_accessed=2**20, transcendentals=cells * ch
        ),
        name="conv",
    )(wide, preact, upstream, kernel, left, right)
    return out, slope, keep, send, (kernel, east, west, left, right)


def input_grad_kernel(
    lat, lon, slope_ref, w_ref, east_ref, west_ref, left_ref, right_ref, xgrad_ref, s_wide
):
    cells, ch = slope_ref.shape
    chunk = cells // 2
    columns = [
        shifted(left_ref[0], east_ref[1], lat),
        shifted(left_ref[1], right_ref[0], lat),
        shifted(west_ref[0], right_ref[1], lat),
    ]
    total = jnp.zeros((2 * lat, ch), F32)
    for a in range(3):
        for b in range(3):
            tap = 3 * a + b
            total += dot(columns[b][a], w_ref[tap * ch : (tap + 1) * ch, :])
    upstream = jnp.concatenate([left_ref[2].astype(F32), right_ref[2].astype(F32)], 0)
    edge = swish(total, upstream)[1].astype(BF16).astype(F32)
    widen(slope_ref, edge[:lat], edge[lat:], s_wide, lat, lon, 2, 0)

    def input_grad(step, carry):
        at = pl.multiple_of(step * chunk, chunk)
        total = None
        for a in range(3):
            for b in range(3):
                tap = 3 * a + b
                term = dot(
                    s_wide[pl.ds(at + (2 - a) * lon, chunk), b * ch : (b + 1) * ch],
                    w_ref[tap * ch : (tap + 1) * ch, :],
                    NT,
                )
                total = term if total is None else total + term
        xgrad_ref[pl.ds(at, chunk), :] = total.astype(BF16)
        return carry

    lax.fori_loop(0, cells // chunk, input_grad, 0)


def matrix_kernel(wgrad_ref, error_ref, q_ref, matrix_ref, p_ref):
    matrix = wgrad_ref[0].astype(F32)
    for t in range(1, wgrad_ref.shape[0]):
        matrix += wgrad_ref[t].astype(F32)
    matrix += error_ref[...]
    matrix_ref[...] = matrix
    q_parts = stacked_parts(q_ref[...])
    p_rows = jnp.zeros(p_ref.shape, F32)
    for part in in_parts(matrix):
        p_rows += fold(dot(q_parts, part, NT), q_ref.shape[0])
    p_ref[...] = p_rows.astype(BF16)


def image_mean(ref):
    total = ref[0].astype(F32)
    for image in range(1, ref.shape[0]):
        total += ref[image].astype(F32)
    return total * (1.0 / ref.shape[0])


def moment_kernel(matrix_ref, p_ref, rows_ref, moment_ref):
    _, rank, rows = p_ref.shape
    ch = matrix_ref.shape[1]
    p_rows = image_mean(p_ref)
    rows_ref[...] = p_rows
    p_parts = stacked_parts(p_rows)
    moment = jnp.zeros((rank, ch), F32)
    for part in in_parts(matrix_ref[...]):
        moment += fold(dot(p_parts, part), rank)
    moment_ref[:, 0:ch] = moment.astype(BF16)
    gram = jnp.zeros((rank, 128), F32)
    for part in in_parts(p_rows):
        thrice = [part.astype(F32)] * 3 + [jnp.zeros((128 - 3 * rank, rows), F32)]
        gram += fold(dot(p_parts, jnp.concatenate(thrice, 0).astype(BF16), NT), rank)
    place = lax.broadcasted_iota(jnp.int32, (rank, 128), 1) // rank
    parts = [part.astype(F32) for part in in_parts(gram)]
    parts = jnp.where(place == 0, parts[0], jnp.where(place == 1, parts[1], parts[2]))
    moment_ref[:, ch : ch + 128] = parts.astype(BF16)


def factor_kernel(gram_ref, p_ref, left_ref, held_ref, solve_ref):
    rank = p_ref.shape[0]
    gram = gram_ref[...]
    gram += pltpu.roll(gram, 128 - rank, 1) + pltpu.roll(gram, 128 - 2 * rank, 1)
    whole = gram
    p_rows = p_ref[...]
    index = lax.broadcasted_iota(jnp.int32, (rank, 1), 0)
    lane = lax.broadcasted_iota(jnp.int32, (rank, 128), 1)
    solve = jnp.where(lane == index, 1.0, 0.0)
    for j in range(rank):
        floor = 1e-14 * whole[j : j + 1, j : j + 1]
        inverse = 1.0 / jnp.sqrt(jnp.maximum(gram[j : j + 1, j : j + 1], floor))
        projected = jnp.where(index > j, gram[:, j : j + 1] * inverse, 0.0)

        def step(value):
            unit = value[j : j + 1, :] * inverse
            return jnp.where(index == j, unit, value - projected * unit)

        gram, p_rows, solve = step(gram), step(p_rows), step(solve)
    left_ref[...] = p_rows
    held_ref[...] = p_rows
    solve_ref[...] = solve


def residual_kernel(matrix_ref, left_ref, solve_ref, s_ref, next_ref, right_ref):
    rank = s_ref.shape[1]
    mean = image_mean(s_ref)
    solve = solve_ref[...]
    right = solve[:, 0:1] * mean[0:1, :]
    for k in range(1, rank):
        right += solve[:, k : k + 1] * mean[k : k + 1, :]
    right_ref[...] = right
    columns = left_ref[...].T
    total = matrix_ref[...]
    for k in range(rank):
        total -= columns[:, k : k + 1] * right[k : k + 1, :]
    next_ref[...] = total


def shift(axis, step):
    count = lax.axis_size(axis)
    return [(i, (i + step) % count) for i in range(count)]


def cores(axis):
    return [(i, i ^ 1) for i in range(lax.axis_size(axis))]


def chips(axis):
    count = lax.axis_size(axis)
    return [list(range(core, count, 2)) for core in range(2)]


def shares_of(value, axis):
    count = lax.axis_size(axis)
    return lax.all_to_all(
        jnp.broadcast_to(value[None], (count,) + value.shape), axis, 0, 0, tiled=True
    )


def per_device(inputs, kernel, cotangent, feedback, q_start):
    _, lat, lon, ch = inputs.shape
    kernel_rows = kernel.shape[0]
    rows_dev = feedback.shape[1]
    rank = q_start.shape[1]
    cells = lat * lon
    tiles = lax.axis_size("tile")
    scale = 1.0 / math.sqrt(cells * tiles)
    x, upstream, error = inputs[0], cotangent[0], feedback[0]

    x_cells, upstream_cells = x.reshape(cells, ch), upstream.reshape(cells, ch)
    sds, local = jax.ShapeDtypeStruct, pltpu.VMEM
    out, slope, keep, send, held = conv_call(
        x_cells, upstream_cells, kernel, lat, lon, tiles, rows_dev, scale
    )
    xgrad = pl.pallas_call(
        functools.partial(input_grad_kernel, lat, lon),
        out_shape=sds((cells, ch), BF16),
        in_specs=[VMEM] * 6,
        out_specs=VMEM,
        scratch_shapes=[pltpu.VMEM((cells + 2 * lon, 3 * ch), BF16)],
        compiler_params=pltpu.CompilerParams(vmem_limit_bytes=BIG),
        cost_estimate=pl.CostEstimate(
            flops=2 * cells * kernel_rows * ch, bytes_accessed=2 * 2**20, transcendentals=0
        ),
        name="input_grad",
    )(slope, *held)

    summed = keep + lax.ppermute(send, "tile", cores("tile"))
    wgrad_rows = lax.all_to_all(
        summed, "tile", 0, 0, axis_index_groups=chips("tile"), tiled=True
    )
    small = pltpu.CompilerParams(vmem_limit_bytes=16 * 2**20)
    matrix, p_local = pl.pallas_call(
        matrix_kernel,
        out_shape=(local((rows_dev, ch), F32), local((rank, rows_dev), BF16)),
        in_specs=[VMEM] * 3,
        out_specs=(VMEM,) * 2,
        compiler_params=small,
        name="matrix",
    )(wgrad_rows, error, q_start.T)
    p_rows, moment = pl.pallas_call(
        moment_kernel,
        out_shape=(local((rank, rows_dev), F32), local((rank, ch + 128), BF16)),
        in_specs=[VMEM] * 2,
        out_specs=(VMEM,) * 2,
        compiler_params=small,
        name="moment",
    )(matrix, shares_of(p_local, "dp"))
    moment = shares_of(moment, "tile").astype(F32).sum(0)
    p_factor, held_factor, solve = pl.pallas_call(
        factor_kernel,
        out_shape=(
            sds((rank, rows_dev), F32),
            local((rank, rows_dev), F32),
            local((rank, 128), F32),
        ),
        in_specs=[VMEM] * 2,
        out_specs=(VMEM,) * 3,
        compiler_params=small,
        name="factor",
    )(moment[:, ch:], p_rows)
    new_feedback, q_factor = pl.pallas_call(
        residual_kernel,
        out_shape=(sds((rows_dev, ch), F32), sds((rank, ch), F32)),
        in_specs=[VMEM] * 4,
        out_specs=(VMEM,) * 2,
        compiler_params=small,
        name="residual",
    )(matrix, held_factor, solve, shares_of(moment[:, :ch].astype(BF16), "dp"))

    shape = inputs.shape
    return (out.reshape(shape), xgrad.reshape(shape), p_factor.T, q_factor.T, new_feedback[None])


def solution(mesh):
    in_specs = (
        P("dp", None, "tile", None),
        P(),
        P("dp", None, "tile", None),
        P("dp", "tile", None),
        P(),
    )
    out_specs = (
        P("dp", None, "tile", None),
        P("dp", None, "tile", None),
        P("tile", None),
        P(),
        P("dp", "tile", None),
    )
    return jax.shard_map(
        per_device, mesh=mesh, in_specs=in_specs, out_specs=out_specs, check_vma=False
    )
```

```python
import functools
import math

import jax
import jax.numpy as jnp
from jax import lax
from jax.experimental import pallas as pl
from jax.experimental.pallas import tpu as pltpu
from jax.sharding import PartitionSpec as P

F32 = jnp.float32
BF16 = jnp.bfloat16
NN = (((1,), (0,)), ((), ()))
NT = (((1,), (1,)), ((), ()))
TN = (((0,), (0,)), ((), ()))
VMEM = pl.BlockSpec(memory_space=pltpu.VMEM)
HBM = pl.BlockSpec(memory_space=pl.ANY)
BIG = 24 * 2**20
WHOLE = 56 * 2**20


def dot(left, right, dims=NN):
    return lax.dot_general(left, right, dims, preferred_element_type=F32)


def in_parts(value):
    parts = []
    for _ in range(3):
        part = value.astype(BF16)
        parts.append(part)
        value = value - part.astype(F32)
    return parts


def stacked_parts(value):
    return jnp.concatenate([part.astype(F32) for part in in_parts(value)], 0).astype(BF16)


def fold(product, rank):
    return product[0:rank] + product[rank : 2 * rank] + product[2 * rank : 3 * rank]


def fetch(pairs, sems):
    copies = [pltpu.make_async_copy(held, place, sems.at[k]) for k, (held, place) in enumerate(pairs)]
    for copy in copies:
        copy.start()
    return copies


def swish(preact, upstream):
    s = jax.nn.sigmoid(preact)
    return preact * s, upstream * s * (1.0 + preact * (1.0 - s))


def widen(source, left, right, wide, lat, lon, low, high):
    ch = source.shape[1]
    rows = 8 * lon
    column = lax.broadcasted_iota(jnp.int32, (rows, ch), 0) & (lon - 1)
    wide[0:lon, :] = jnp.zeros((lon, 3 * ch), BF16)
    wide[lon + lat * lon :, :] = jnp.zeros((lon, 3 * ch), BF16)
    for step in range(lat // 8):
        value = source[step * rows : (step + 1) * rows, :]
        wider = value.astype(F32)
        edges = [spread(edge, step, lon) for edge in (left, right)]
        west = jnp.where(column == 0, edges[0], pltpu.roll(wider, 1, 0))
        east = jnp.where(column == lon - 1, edges[1], pltpu.roll(wider, rows - 1, 0))
        at = slice(lon + step * rows, lon + (step + 1) * rows)
        wide[at, low * ch : (low + 1) * ch] = west.astype(BF16)
        wide[at, ch : 2 * ch] = value
        wide[at, high * ch : (high + 1) * ch] = east.astype(BF16)


def spread(edge, step, lon):
    if edge is None:
        return 0.0
    ch = edge.shape[1]
    part = edge[step * 8 : step * 8 + 8, None, :]
    return jnp.broadcast_to(part, (8, lon, ch)).reshape(8 * lon, ch)


def picked(columns, source, lat, lon):
    shape = (lat * len(columns), lat * lon)
    cell = lax.broadcasted_iota(jnp.int32, shape, 1)
    row = lax.broadcasted_iota(jnp.int32, shape, 0)
    target = (row & (lat - 1)) * lon
    for k, column in enumerate(columns):
        target = jnp.where((row >= k * lat) & (row < (k + 1) * lat), target + column, target)
    return dot((cell == target).astype(F32).astype(BF16), source[...]).astype(BF16)


def load_kernel(
    lat, lon, x_hbm, cot_hbm, w_hbm, x_ref, cot_ref, w_ref, east_ref, west_ref, sems
):
    x_copy, cot_copy, w_copy = fetch([(x_hbm, x_ref), (cot_hbm, cot_ref), (w_hbm, w_ref)], sems)
    x_copy.wait()
    x_edge = picked((0, 1, lon - 2, lon - 1), x_ref, lat, lon)
    west_ref[0] = x_edge[0:lat]
    west_ref[1] = x_edge[lat : 2 * lat]
    east_ref[0] = x_edge[2 * lat : 3 * lat]
    east_ref[1] = x_edge[3 * lat : 4 * lat]
    cot_copy.wait()
    cot_edge = picked((0, lon - 1), cot_ref, lat, lon)
    west_ref[2] = cot_edge[0:lat]
    east_ref[2] = cot_edge[lat : 2 * lat]
    w_copy.wait()


def inner_kernel(lat, lon, x_ref, w_ref, x_wide, preact_ref):
    cells, ch = x_ref.shape
    chunk = cells // 2
    widen(x_ref, None, None, x_wide, lat, lon, 0, 2)

    def forward(step, carry):
        at = pl.multiple_of(step * chunk, chunk)
        total = dot(x_wide[pl.ds(at, chunk), :], w_ref[0 : 3 * ch, :])
        total += dot(x_wide[pl.ds(at + lon, chunk), :], w_ref[3 * ch : 6 * ch, :])
        total += dot(x_wide[pl.ds(at + 2 * lon, chunk), :], w_ref[6 * ch : 9 * ch, :])
        preact_ref[pl.ds(at, chunk), :] = total
        return carry

    lax.fori_loop(0, cells // chunk, forward, 0)


def shifted(west, east, lat):
    value = jnp.concatenate([west.astype(F32), east.astype(F32)], 0)
    row = lax.broadcasted_iota(jnp.int32, value.shape, 0) & (lat - 1)
    south = jnp.where(row == 0, 0.0, pltpu.roll(value, 1, 0))
    north = jnp.where(row == lat - 1, 0.0, pltpu.roll(value, 2 * lat - 1, 0))
    return [south.astype(BF16), value.astype(BF16), north.astype(BF16)]


def conv_kernel(
    lat, lon, scale, x_wide, preact_ref, cot_ref, w_ref, left_ref, right_ref,
    out_ref, slope_ref, keep_ref, send_ref, x_sides, wgrad_ref,
):
    cells, ch = cot_ref.shape
    core = lax.axis_index("tile") & 1
    tap = lambda k: w_ref[k * ch : (k + 1) * ch, :]

    beside = shifted(left_ref[1], right_ref[0], lat)

    west = sum(dot(beside[a][0:lat], tap(3 * a)) for a in range(3))
    east = sum(dot(beside[a][lat : 2 * lat], tap(3 * a + 2)) for a in range(3))
    rows = 8 * lon
    column = lax.broadcasted_iota(jnp.int32, (rows, ch), 0) & (lon - 1)
    for step in range(lat // 8):
        at = slice(step * rows, (step + 1) * rows)
        preact = preact_ref[at, :]
        preact += jnp.where(column == 0, spread(west, step, lon), 0.0)
        preact += jnp.where(column == lon - 1, spread(east, step, lon), 0.0)
        out, slope = swish(preact, cot_ref[at, :].astype(F32))
        out_ref[at, :] = out.astype(BF16)
        slope_ref[at, :] = slope.astype(BF16)
        wide_at = slice(lon + step * rows, lon + (step + 1) * rows)
        for side, place, edge in ((0, 0, left_ref[1]), (1, lon - 1, right_ref[0])):
            value = x_wide[wide_at, 2 * side * ch : (2 * side + 1) * ch].astype(F32)
            value = jnp.where(column == place, spread(edge.astype(F32), step, lon), value)
            x_sides[wide_at, side * ch : (side + 1) * ch] = value.astype(BF16)
    x_sides[0:lon, :] = jnp.zeros((lon, 2 * ch), BF16)
    x_sides[lon + cells :, :] = jnp.zeros((lon, 2 * ch), BF16)

    for k in range(9):
        a, b = k // 3, k % 3
        source, block = (x_wide, 1) if b == 1 else (x_sides, b // 2)
        term = dot(
            source[a * lon : a * lon + cells, block * ch : (block + 1) * ch], slope_ref[...], TN
        )
        wgrad_ref[k * ch : (k + 1) * ch, :] = (term * scale).astype(BF16)
    pairs, piece, _ = keep_ref.shape
    for pair in range(pairs):
        for held, owner in ((keep_ref, core), (send_ref, 1 - core)):
            start = pl.multiple_of((2 * pair + owner) * piece, 16)
            held[pair] = wgrad_ref[pl.ds(start, piece), :]


def conv_call(x, upstream, kernel, lat, lon, tiles, rows_dev, scale):
    cells, ch = x.shape
    kernel_rows = kernel.shape[0]
    sds, local = jax.ShapeDtypeStruct, pltpu.VMEM
    image = local((cells, ch), BF16)
    edges = local((3, lat, ch), BF16)
    x, upstream, kernel, east, west = pl.pallas_call(
        functools.partial(load_kernel, lat, lon),
        out_shape=(image, image, local((kernel_rows, ch), BF16), edges, edges),
        in_specs=[HBM] * 3,
        out_specs=(VMEM,) * 5,
        scratch_shapes=[pltpu.SemaphoreType.DMA((3,))],
        compiler_params=pltpu.CompilerParams(vmem_limit_bytes=WHOLE),
        name="load",
    )(x, upstream, kernel)
    left = lax.ppermute(east, "tile", shift("tile", 1))
    right = lax.ppermute(west, "tile", shift("tile", -1))
    wide, preact = pl.pallas_call(
        functools.partial(inner_kernel, lat, lon),
        out_shape=(local((cells + 2 * lon, 3 * ch), BF16), local((cells, ch), F32)),
        in_specs=[VMEM] * 2,
        out_specs=(VMEM,) * 2,
        compiler_params=pltpu.CompilerParams(vmem_limit_bytes=BIG),
        cost_estimate=pl.CostEstimate(
            flops=2 * cells * kernel_rows * ch, bytes_accessed=0, transcendentals=0
        ),
        name="inner",
    )(x, kernel)
    half = local((tiles // 2, rows_dev, ch), BF16)
    out, slope, keep, send = pl.pallas_call(
        functools.partial(conv_kernel, lat, lon, scale),
        out_shape=(image, image, half, half),
        in_specs=[VMEM] * 6,
        out_specs=(VMEM,) * 4,
        scratch_shapes=[
            pltpu.VMEM((cells + 2 * lon, 2 * ch), BF16),
            pltpu.VMEM((kernel_rows, ch), BF16),
        ],
        compiler_params=pltpu.CompilerParams(vmem_limit_bytes=BIG),
        cost_estimate=pl.CostEstimate(
            flops=2 * cells * kernel_rows * ch, bytes_accessed=2**20, transcendentals=cells * ch
        ),
        name="conv",
    )(wide, preact, upstream, kernel, left, right)
    return out, slope, keep, send, (kernel, east, west, left, right)


def input_grad_kernel(
    lat, lon, out_ref, slope_ref, w_ref, east_ref, west_ref, left_ref, right_ref, out_hbm, xgrad_ref,
    s_wide, out_sem,
):
    cells, ch = slope_ref.shape
    out_copy = pltpu.make_async_copy(out_ref, out_hbm, out_sem)
    out_copy.start()
    chunk = cells // 2
    columns = [
        shifted(left_ref[0], east_ref[1], lat),
        shifted(left_ref[1], right_ref[0], lat),
        shifted(west_ref[0], right_ref[1], lat),
    ]
    total = jnp.zeros((2 * lat, ch), F32)
    for a in range(3):
        for b in range(3):
            tap = 3 * a + b
            total += dot(columns[b][a], w_ref[tap * ch : (tap + 1) * ch, :])
    upstream = jnp.concatenate([left_ref[2].astype(F32), right_ref[2].astype(F32)], 0)
    edge = swish(total, upstream)[1].astype(BF16).astype(F32)
    widen(slope_ref, edge[:lat], edge[lat:], s_wide, lat, lon, 2, 0)

    def input_grad(step, carry):
        at = pl.multiple_of(step * chunk, chunk)
        total = None
        for a in range(3):
            for b in range(3):
                tap = 3 * a + b
                term = dot(
                    s_wide[pl.ds(at + (2 - a) * lon, chunk), b * ch : (b + 1) * ch],
                    w_ref[tap * ch : (tap + 1) * ch, :],
                    NT,
                )
                total = term if total is None else total + term
        xgrad_ref[pl.ds(at, chunk), :] = total.astype(BF16)
        return carry

    lax.fori_loop(0, cells // chunk, input_grad, 0)
    out_copy.wait()


def matrix_kernel(wgrad_ref, error_ref, q_ref, matrix_ref, p_ref):
    matrix = wgrad_ref[0].astype(F32)
    for t in range(1, wgrad_ref.shape[0]):
        matrix += wgrad_ref[t].astype(F32)
    matrix += error_ref[...]
    matrix_ref[...] = matrix
    q_parts = stacked_parts(q_ref[...])
    p_rows = jnp.zeros(p_ref.shape, F32)
    for part in in_parts(matrix):
        p_rows += fold(dot(q_parts, part, NT), q_ref.shape[0])
    p_ref[...] = p_rows.astype(BF16)


def image_mean(ref):
    total = ref[0].astype(F32)
    for image in range(1, ref.shape[0]):
        total += ref[image].astype(F32)
    return total * (1.0 / ref.shape[0])


def moment_kernel(matrix_ref, p_ref, rows_ref, moment_ref):
    _, rank, rows = p_ref.shape
    ch = matrix_ref.shape[1]
    p_rows = image_mean(p_ref)
    rows_ref[...] = p_rows
    p_parts = stacked_parts(p_rows)
    moment = jnp.zeros((rank, ch), F32)
    for part in in_parts(matrix_ref[...]):
        moment += fold(dot(p_parts, part), rank)
    moment_ref[:, 0:ch] = moment.astype(BF16)
    gram = jnp.zeros((rank, 128), F32)
    for part in in_parts(p_rows):
        thrice = [part.astype(F32)] * 3 + [jnp.zeros((128 - 3 * rank, rows), F32)]
        gram += fold(dot(p_parts, jnp.concatenate(thrice, 0).astype(BF16), NT), rank)
    place = lax.broadcasted_iota(jnp.int32, (rank, 128), 1) // rank
    parts = [part.astype(F32) for part in in_parts(gram)]
    parts = jnp.where(place == 0, parts[0], jnp.where(place == 1, parts[1], parts[2]))
    moment_ref[:, ch : ch + 128] = parts.astype(BF16)


def factor_kernel(gram_ref, p_ref, left_ref, columns_ref, solve_ref):
    rank = p_ref.shape[0]
    gram = gram_ref[...]
    gram += pltpu.roll(gram, 128 - rank, 1) + pltpu.roll(gram, 128 - 2 * rank, 1)
    whole = gram
    p_rows = p_ref[...]
    index = lax.broadcasted_iota(jnp.int32, (rank, 1), 0)
    lane = lax.broadcasted_iota(jnp.int32, (rank, 128), 1)
    solve = jnp.where(lane == index, 1.0, 0.0)
    for j in range(rank):
        floor = 1e-14 * whole[j : j + 1, j : j + 1]
        inverse = 1.0 / jnp.sqrt(jnp.maximum(gram[j : j + 1, j : j + 1], floor))
        projected = jnp.where(index > j, gram[:, j : j + 1] * inverse, 0.0)

        def step(value):
            unit = value[j : j + 1, :] * inverse
            return jnp.where(index == j, unit, value - projected * unit)

        gram, p_rows, solve = step(gram), step(p_rows), step(solve)
    left_ref[...] = p_rows
    columns_ref[...] = p_rows.T
    solve_ref[...] = solve


def residual_kernel(matrix_ref, columns_ref, solve_ref, s_ref, next_ref, right_ref):
    rank = s_ref.shape[1]
    mean = image_mean(s_ref)
    solve = solve_ref[...]
    right = solve[:, 0:1] * mean[0:1, :]
    for k in range(1, rank):
        right += solve[:, k : k + 1] * mean[k : k + 1, :]
    right_ref[...] = right
    columns = columns_ref[...]
    total = matrix_ref[...]
    for k in range(rank):
        total -= columns[:, k : k + 1] * right[k : k + 1, :]
    next_ref[...] = total


def shift(axis, step):
    count = lax.axis_size(axis)
    return [(i, (i + step) % count) for i in range(count)]


def cores(axis):
    return [(i, i ^ 1) for i in range(lax.axis_size(axis))]


def chips(axis):
    count = lax.axis_size(axis)
    return [list(range(core, count, 2)) for core in range(2)]


def shares_of(value, axis):
    count = lax.axis_size(axis)
    return lax.all_to_all(
        jnp.broadcast_to(value[None], (count,) + value.shape), axis, 0, 0, tiled=True
    )


def per_device(inputs, kernel, cotangent, feedback, q_start):
    _, lat, lon, ch = inputs.shape
    kernel_rows = kernel.shape[0]
    rows_dev = feedback.shape[1]
    rank = q_start.shape[1]
    cells = lat * lon
    tiles = lax.axis_size("tile")
    scale = 1.0 / math.sqrt(cells * tiles)
    x, upstream, error = inputs[0], cotangent[0], feedback[0]

    x_cells, upstream_cells = x.reshape(cells, ch), upstream.reshape(cells, ch)
    sds, local = jax.ShapeDtypeStruct, pltpu.VMEM
    out, slope, keep, send, held = conv_call(
        x_cells, upstream_cells, kernel, lat, lon, tiles, rows_dev, scale
    )
    out, xgrad = pl.pallas_call(
        functools.partial(input_grad_kernel, lat, lon),
        out_shape=(sds((cells, ch), BF16),) * 2,
        in_specs=[VMEM] * 7,
        out_specs=(HBM, VMEM),
        scratch_shapes=[
            pltpu.VMEM((cells + 2 * lon, 3 * ch), BF16),
            pltpu.SemaphoreType.DMA,
        ],
        compiler_params=pltpu.CompilerParams(vmem_limit_bytes=BIG),
        cost_estimate=pl.CostEstimate(
            flops=2 * cells * kernel_rows * ch, bytes_accessed=2 * 2**20, transcendentals=0
        ),
        name="input_grad",
    )(out, slope, *held)

    summed = keep + lax.ppermute(send, "tile", cores("tile"))
    wgrad_rows = lax.all_to_all(
        summed, "tile", 0, 0, axis_index_groups=chips("tile"), tiled=True
    )
    small = pltpu.CompilerParams(vmem_limit_bytes=16 * 2**20)
    matrix, p_local = pl.pallas_call(
        matrix_kernel,
        out_shape=(local((rows_dev, ch), F32), local((rank, rows_dev), BF16)),
        in_specs=[VMEM] * 3,
        out_specs=(VMEM,) * 2,
        compiler_params=small,
        name="matrix",
    )(wgrad_rows, error, q_start.T)
    p_rows, moment = pl.pallas_call(
        moment_kernel,
        out_shape=(local((rank, rows_dev), F32), local((rank, ch + 128), BF16)),
        in_specs=[VMEM] * 2,
        out_specs=(VMEM,) * 2,
        compiler_params=small,
        name="moment",
    )(matrix, shares_of(p_local, "dp"))
    moment = shares_of(moment, "tile").astype(F32).sum(0)
    p_factor, columns, solve = pl.pallas_call(
        factor_kernel,
        out_shape=(
            sds((rank, rows_dev), F32),
            local((rows_dev, rank), F32),
            local((rank, 128), F32),
        ),
        in_specs=[VMEM] * 2,
        out_specs=(VMEM,) * 3,
        compiler_params=small,
        name="factor",
    )(moment[:, ch:], p_rows)
    new_feedback, q_factor = pl.pallas_call(
        residual_kernel,
        out_shape=(sds((rows_dev, ch), F32), sds((rank, ch), F32)),
        in_specs=[VMEM] * 4,
        out_specs=(VMEM,) * 2,
        compiler_params=small,
        name="residual",
    )(matrix, columns, solve, shares_of(moment[:, :ch].astype(BF16), "dp"))

    shape = inputs.shape
    return (out.reshape(shape), xgrad.reshape(shape), p_factor.T, q_factor.T, new_feedback[None])


def solution(mesh):
    in_specs = (
        P("dp", None, "tile", None),
        P(),
        P("dp", None, "tile", None),
        P("dp", "tile", None),
        P(),
    )
    out_specs = (
        P("dp", None, "tile", None),
        P("dp", None, "tile", None),
        P("tile", None),
        P(),
        P("dp", "tile", None),
    )
    return jax.shard_map(
        per_device, mesh=mesh, in_specs=in_specs, out_specs=out_specs, check_vma=False
    )
```

```python
import functools
import math

import jax
import jax.numpy as jnp
from jax import lax
from jax.experimental import pallas as pl
from jax.experimental.pallas import tpu as pltpu
from jax.sharding import PartitionSpec as P

F32 = jnp.float32
BF16 = jnp.bfloat16
NN = (((1,), (0,)), ((), ()))
NT = (((1,), (1,)), ((), ()))
TN = (((0,), (0,)), ((), ()))
VMEM = pl.BlockSpec(memory_space=pltpu.VMEM)
HBM = pl.BlockSpec(memory_space=pl.ANY)
BIG = 24 * 2**20
WHOLE = 56 * 2**20


def dot(left, right, dims=NN):
    return lax.dot_general(left, right, dims, preferred_element_type=F32)


def in_parts(value):
    parts = []
    for _ in range(3):
        part = value.astype(BF16)
        parts.append(part)
        value = value - part.astype(F32)
    return parts


def stacked_parts(value):
    return jnp.concatenate([part.astype(F32) for part in in_parts(value)], 0).astype(BF16)


def fold(product, rank):
    return product[0:rank] + product[rank : 2 * rank] + product[2 * rank : 3 * rank]


def fetch(pairs, sems):
    copies = [pltpu.make_async_copy(held, place, sems.at[k]) for k, (held, place) in enumerate(pairs)]
    for copy in copies:
        copy.start()
    return copies


def swish(preact, upstream):
    s = jax.nn.sigmoid(preact)
    return preact * s, upstream * s * (1.0 + preact * (1.0 - s))


def widen(source, left, right, wide, lat, lon, low, high):
    ch = source.shape[1]
    rows = 8 * lon
    column = lax.broadcasted_iota(jnp.int32, (rows, ch), 0) & (lon - 1)
    wide[0:lon, :] = jnp.zeros((lon, 3 * ch), BF16)
    wide[lon + lat * lon :, :] = jnp.zeros((lon, 3 * ch), BF16)
    for step in range(lat // 8):
        value = source[step * rows : (step + 1) * rows, :]
        wider = value.astype(F32)
        edges = [spread(edge, step, lon) for edge in (left, right)]
        west = jnp.where(column == 0, edges[0], pltpu.roll(wider, 1, 0))
        east = jnp.where(column == lon - 1, edges[1], pltpu.roll(wider, rows - 1, 0))
        at = slice(lon + step * rows, lon + (step + 1) * rows)
        wide[at, low * ch : (low + 1) * ch] = west.astype(BF16)
        wide[at, ch : 2 * ch] = value
        wide[at, high * ch : (high + 1) * ch] = east.astype(BF16)


def spread(edge, step, lon):
    if edge is None:
        return 0.0
    ch = edge.shape[1]
    part = edge[step * 8 : step * 8 + 8, None, :]
    return jnp.broadcast_to(part, (8, lon, ch)).reshape(8 * lon, ch)


def picked(columns, source, lat, lon):
    shape = (lat * len(columns), lat * lon)
    cell = lax.broadcasted_iota(jnp.int32, shape, 1)
    row = lax.broadcasted_iota(jnp.int32, shape, 0)
    target = (row & (lat - 1)) * lon
    for k, column in enumerate(columns):
        target = jnp.where((row >= k * lat) & (row < (k + 1) * lat), target + column, target)
    return dot((cell == target).astype(F32).astype(BF16), source[...]).astype(BF16)


def load_kernel(
    lat, lon, x_hbm, cot_hbm, w_hbm, x_ref, cot_ref, w_ref, east_ref, west_ref, sems
):
    x_copy, cot_copy, w_copy = fetch([(x_hbm, x_ref), (cot_hbm, cot_ref), (w_hbm, w_ref)], sems)
    x_copy.wait()
    x_edge = picked((0, 1, lon - 2, lon - 1), x_ref, lat, lon)
    west_ref[0] = x_edge[0:lat]
    west_ref[1] = x_edge[lat : 2 * lat]
    east_ref[0] = x_edge[2 * lat : 3 * lat]
    east_ref[1] = x_edge[3 * lat : 4 * lat]
    cot_copy.wait()
    cot_edge = picked((0, lon - 1), cot_ref, lat, lon)
    west_ref[2] = cot_edge[0:lat]
    east_ref[2] = cot_edge[lat : 2 * lat]
    w_copy.wait()


def inner_kernel(lat, lon, x_ref, w_ref, x_wide, preact_ref):
    cells, ch = x_ref.shape
    chunk = cells // 2
    widen(x_ref, None, None, x_wide, lat, lon, 0, 2)

    def forward(step, carry):
        at = pl.multiple_of(step * chunk, chunk)
        total = dot(x_wide[pl.ds(at, chunk), :], w_ref[0 : 3 * ch, :])
        total += dot(x_wide[pl.ds(at + lon, chunk), :], w_ref[3 * ch : 6 * ch, :])
        total += dot(x_wide[pl.ds(at + 2 * lon, chunk), :], w_ref[6 * ch : 9 * ch, :])
        preact_ref[pl.ds(at, chunk), :] = total
        return carry

    lax.fori_loop(0, cells // chunk, forward, 0)


def shifted(west, east, lat):
    value = jnp.concatenate([west.astype(F32), east.astype(F32)], 0)
    row = lax.broadcasted_iota(jnp.int32, value.shape, 0) & (lat - 1)
    south = jnp.where(row == 0, 0.0, pltpu.roll(value, 1, 0))
    north = jnp.where(row == lat - 1, 0.0, pltpu.roll(value, 2 * lat - 1, 0))
    return [south.astype(BF16), value.astype(BF16), north.astype(BF16)]


def conv_kernel(
    lat, lon, scale, x_wide, preact_ref, cot_ref, w_ref, left_ref, right_ref,
    out_ref, slope_ref, keep_ref, send_ref, x_sides, wgrad_ref,
):
    cells, ch = cot_ref.shape
    core = lax.axis_index("tile") & 1
    tap = lambda k: w_ref[k * ch : (k + 1) * ch, :]

    beside = shifted(left_ref[1], right_ref[0], lat)

    west = sum(dot(beside[a][0:lat], tap(3 * a)) for a in range(3))
    east = sum(dot(beside[a][lat : 2 * lat], tap(3 * a + 2)) for a in range(3))
    rows = 8 * lon
    column = lax.broadcasted_iota(jnp.int32, (rows, ch), 0) & (lon - 1)
    for step in range(lat // 8):
        at = slice(step * rows, (step + 1) * rows)
        preact = preact_ref[at, :]
        preact += jnp.where(column == 0, spread(west, step, lon), 0.0)
        preact += jnp.where(column == lon - 1, spread(east, step, lon), 0.0)
        out, slope = swish(preact, cot_ref[at, :].astype(F32))
        out_ref[at, :] = out.astype(BF16)
        slope_ref[at, :] = slope.astype(BF16)
        wide_at = slice(lon + step * rows, lon + (step + 1) * rows)
        for side, place, edge in ((0, 0, left_ref[1]), (1, lon - 1, right_ref[0])):
            value = x_wide[wide_at, 2 * side * ch : (2 * side + 1) * ch].astype(F32)
            value = jnp.where(column == place, spread(edge.astype(F32), step, lon), value)
            x_sides[wide_at, side * ch : (side + 1) * ch] = value.astype(BF16)
    x_sides[0:lon, :] = jnp.zeros((lon, 2 * ch), BF16)
    x_sides[lon + cells :, :] = jnp.zeros((lon, 2 * ch), BF16)

    for k in range(9):
        a, b = k // 3, k % 3
        source, block = (x_wide, 1) if b == 1 else (x_sides, b // 2)
        term = dot(
            source[a * lon : a * lon + cells, block * ch : (block + 1) * ch], slope_ref[...], TN
        )
        wgrad_ref[k * ch : (k + 1) * ch, :] = (term * scale).astype(BF16)
    pairs, piece, _ = keep_ref.shape

    def divide(own):
        for pair in range(pairs):
            for held, owner in ((keep_ref, own), (send_ref, 1 - own)):
                start = (2 * pair + owner) * piece
                held[pair] = wgrad_ref[start : start + piece, :]

    for own in range(2):
        pl.when(core == own)(functools.partial(divide, own))


def conv_call(x, upstream, kernel, lat, lon, tiles, rows_dev, scale):
    cells, ch = x.shape
    kernel_rows = kernel.shape[0]
    sds, local = jax.ShapeDtypeStruct, pltpu.VMEM
    image = local((cells, ch), BF16)
    edges = local((3, lat, ch), BF16)
    x, upstream, kernel, east, west = pl.pallas_call(
        functools.partial(load_kernel, lat, lon),
        out_shape=(image, image, local((kernel_rows, ch), BF16), edges, edges),
        in_specs=[HBM] * 3,
        out_specs=(VMEM,) * 5,
        scratch_shapes=[pltpu.SemaphoreType.DMA((3,))],
        compiler_params=pltpu.CompilerParams(vmem_limit_bytes=WHOLE),
        name="load",
    )(x, upstream, kernel)
    left = lax.ppermute(east, "tile", shift("tile", 1))
    right = lax.ppermute(west, "tile", shift("tile", -1))
    wide, preact = pl.pallas_call(
        functools.partial(inner_kernel, lat, lon),
        out_shape=(local((cells + 2 * lon, 3 * ch), BF16), local((cells, ch), F32)),
        in_specs=[VMEM] * 2,
        out_specs=(VMEM,) * 2,
        compiler_params=pltpu.CompilerParams(vmem_limit_bytes=BIG),
        cost_estimate=pl.CostEstimate(
            flops=2 * cells * kernel_rows * ch, bytes_accessed=0, transcendentals=0
        ),
        name="inner",
    )(x, kernel)
    half = local((tiles // 2, rows_dev, ch), BF16)
    out, slope, keep, send = pl.pallas_call(
        functools.partial(conv_kernel, lat, lon, scale),
        out_shape=(image, image, half, half),
        in_specs=[VMEM] * 6,
        out_specs=(VMEM,) * 4,
        scratch_shapes=[
            pltpu.VMEM((cells + 2 * lon, 2 * ch), BF16),
            pltpu.VMEM((kernel_rows, ch), BF16),
        ],
        compiler_params=pltpu.CompilerParams(vmem_limit_bytes=BIG),
        cost_estimate=pl.CostEstimate(
            flops=2 * cells * kernel_rows * ch, bytes_accessed=2**20, transcendentals=cells * ch
        ),
        name="conv",
    )(wide, preact, upstream, kernel, left, right)
    return out, slope, keep, send, (kernel, east, west, left, right)


def input_grad_kernel(
    lat, lon, out_ref, slope_ref, w_ref, east_ref, west_ref, left_ref, right_ref, out_hbm, xgrad_ref,
    s_wide, out_sem,
):
    cells, ch = slope_ref.shape
    out_copy = pltpu.make_async_copy(out_ref, out_hbm, out_sem)
    out_copy.start()
    chunk = cells // 2
    columns = [
        shifted(left_ref[0], east_ref[1], lat),
        shifted(left_ref[1], right_ref[0], lat),
        shifted(west_ref[0], right_ref[1], lat),
    ]
    total = jnp.zeros((2 * lat, ch), F32)
    for a in range(3):
        for b in range(3):
            tap = 3 * a + b
            total += dot(columns[b][a], w_ref[tap * ch : (tap + 1) * ch, :])
    upstream = jnp.concatenate([left_ref[2].astype(F32), right_ref[2].astype(F32)], 0)
    edge = swish(total, upstream)[1].astype(BF16).astype(F32)
    widen(slope_ref, edge[:lat], edge[lat:], s_wide, lat, lon, 2, 0)

    def input_grad(step, carry):
        at = pl.multiple_of(step * chunk, chunk)
        total = None
        for a in range(3):
            for b in range(3):
                tap = 3 * a + b
                term = dot(
                    s_wide[pl.ds(at + (2 - a) * lon, chunk), b * ch : (b + 1) * ch],
                    w_ref[tap * ch : (tap + 1) * ch, :],
                    NT,
                )
                total = term if total is None else total + term
        xgrad_ref[pl.ds(at, chunk), :] = total.astype(BF16)
        return carry

    lax.fori_loop(0, cells // chunk, input_grad, 0)
    out_copy.wait()


def matrix_kernel(wgrad_ref, error_ref, q_ref, matrix_ref, p_ref):
    matrix = wgrad_ref[0].astype(F32)
    for t in range(1, wgrad_ref.shape[0]):
        matrix += wgrad_ref[t].astype(F32)
    matrix += error_ref[...]
    matrix_ref[...] = matrix
    q_parts = stacked_parts(q_ref[...])
    p_rows = jnp.zeros(p_ref.shape, F32)
    for part in in_parts(matrix):
        p_rows += fold(dot(q_parts, part, NT), q_ref.shape[0])
    p_ref[...] = p_rows.astype(BF16)


def image_mean(ref):
    total = ref[0].astype(F32)
    for image in range(1, ref.shape[0]):
        total += ref[image].astype(F32)
    return total * (1.0 / ref.shape[0])


def moment_kernel(matrix_ref, p_ref, rows_ref, moment_ref):
    _, rank, rows = p_ref.shape
    ch = matrix_ref.shape[1]
    p_rows = image_mean(p_ref)
    rows_ref[...] = p_rows
    p_parts = stacked_parts(p_rows)
    moment = jnp.zeros((rank, ch), F32)
    for part in in_parts(matrix_ref[...]):
        moment += fold(dot(p_parts, part), rank)
    moment_ref[:, 0:ch] = moment.astype(BF16)
    gram = jnp.zeros((rank, 128), F32)
    for part in in_parts(p_rows):
        thrice = [part.astype(F32)] * 3 + [jnp.zeros((128 - 3 * rank, rows), F32)]
        gram += fold(dot(p_parts, jnp.concatenate(thrice, 0).astype(BF16), NT), rank)
    place = lax.broadcasted_iota(jnp.int32, (rank, 128), 1) // rank
    parts = [part.astype(F32) for part in in_parts(gram)]
    parts = jnp.where(place == 0, parts[0], jnp.where(place == 1, parts[1], parts[2]))
    moment_ref[:, ch : ch + 128] = parts.astype(BF16)


def factor_kernel(gram_ref, p_ref, left_ref, columns_ref, solve_ref):
    rank = p_ref.shape[0]
    gram = gram_ref[...]
    gram += pltpu.roll(gram, 128 - rank, 1) + pltpu.roll(gram, 128 - 2 * rank, 1)
    whole = gram
    p_rows = p_ref[...]
    index = lax.broadcasted_iota(jnp.int32, (rank, 1), 0)
    lane = lax.broadcasted_iota(jnp.int32, (rank, 128), 1)
    solve = jnp.where(lane == index, 1.0, 0.0)
    for j in range(rank):
        floor = 1e-14 * whole[j : j + 1, j : j + 1]
        inverse = 1.0 / jnp.sqrt(jnp.maximum(gram[j : j + 1, j : j + 1], floor))
        projected = jnp.where(index > j, gram[:, j : j + 1] * inverse, 0.0)

        def step(value):
            unit = value[j : j + 1, :] * inverse
            return jnp.where(index == j, unit, value - projected * unit)

        gram, p_rows, solve = step(gram), step(p_rows), step(solve)
    left_ref[...] = p_rows
    columns_ref[...] = p_rows.T
    solve_ref[...] = solve


def residual_kernel(matrix_ref, columns_ref, solve_ref, s_ref, next_ref, right_ref):
    rank = s_ref.shape[1]
    mean = image_mean(s_ref)
    solve = solve_ref[...]
    right = solve[:, 0:1] * mean[0:1, :]
    for k in range(1, rank):
        right += solve[:, k : k + 1] * mean[k : k + 1, :]
    right_ref[...] = right
    columns = columns_ref[...]
    total = matrix_ref[...]
    for k in range(rank):
        total -= columns[:, k : k + 1] * right[k : k + 1, :]
    next_ref[...] = total


def shift(axis, step):
    count = lax.axis_size(axis)
    return [(i, (i + step) % count) for i in range(count)]


def cores(axis):
    return [(i, i ^ 1) for i in range(lax.axis_size(axis))]


def chips(axis):
    count = lax.axis_size(axis)
    return [list(range(core, count, 2)) for core in range(2)]


def shares_of(value, axis):
    count = lax.axis_size(axis)
    return lax.all_to_all(
        jnp.broadcast_to(value[None], (count,) + value.shape), axis, 0, 0, tiled=True
    )


def per_device(inputs, kernel, cotangent, feedback, q_start):
    _, lat, lon, ch = inputs.shape
    kernel_rows = kernel.shape[0]
    rows_dev = feedback.shape[1]
    rank = q_start.shape[1]
    cells = lat * lon
    tiles = lax.axis_size("tile")
    scale = 1.0 / math.sqrt(cells * tiles)
    x, upstream, error = inputs[0], cotangent[0], feedback[0]

    x_cells, upstream_cells = x.reshape(cells, ch), upstream.reshape(cells, ch)
    sds, local = jax.ShapeDtypeStruct, pltpu.VMEM
    out, slope, keep, send, held = conv_call(
        x_cells, upstream_cells, kernel, lat, lon, tiles, rows_dev, scale
    )
    out, xgrad = pl.pallas_call(
        functools.partial(input_grad_kernel, lat, lon),
        out_shape=(sds((cells, ch), BF16),) * 2,
        in_specs=[VMEM] * 7,
        out_specs=(HBM, VMEM),
        scratch_shapes=[
            pltpu.VMEM((cells + 2 * lon, 3 * ch), BF16),
            pltpu.SemaphoreType.DMA,
        ],
        compiler_params=pltpu.CompilerParams(vmem_limit_bytes=BIG),
        cost_estimate=pl.CostEstimate(
            flops=2 * cells * kernel_rows * ch, bytes_accessed=2 * 2**20, transcendentals=0
        ),
        name="input_grad",
    )(out, slope, *held)

    summed = keep + lax.ppermute(send, "tile", cores("tile"))
    wgrad_rows = lax.all_to_all(
        summed, "tile", 0, 0, axis_index_groups=chips("tile"), tiled=True
    )
    small = pltpu.CompilerParams(vmem_limit_bytes=16 * 2**20)
    matrix, p_local = pl.pallas_call(
        matrix_kernel,
        out_shape=(local((rows_dev, ch), F32), local((rank, rows_dev), BF16)),
        in_specs=[VMEM] * 3,
        out_specs=(VMEM,) * 2,
        compiler_params=small,
        name="matrix",
    )(wgrad_rows, error, q_start.T)
    p_rows, moment = pl.pallas_call(
        moment_kernel,
        out_shape=(local((rank, rows_dev), F32), local((rank, ch + 128), BF16)),
        in_specs=[VMEM] * 2,
        out_specs=(VMEM,) * 2,
        compiler_params=small,
        name="moment",
    )(matrix, shares_of(p_local, "dp"))
    moment = shares_of(moment, "tile").astype(F32).sum(0)
    p_factor, columns, solve = pl.pallas_call(
        factor_kernel,
        out_shape=(
            sds((rank, rows_dev), F32),
            local((rows_dev, rank), F32),
            local((rank, 128), F32),
        ),
        in_specs=[VMEM] * 2,
        out_specs=(VMEM,) * 3,
        compiler_params=small,
        name="factor",
    )(moment[:, ch:], p_rows)
    new_feedback, q_factor = pl.pallas_call(
        residual_kernel,
        out_shape=(sds((rows_dev, ch), F32), sds((rank, ch), F32)),
        in_specs=[VMEM] * 4,
        out_specs=(VMEM,) * 2,
        compiler_params=small,
        name="residual",
    )(matrix, columns, solve, shares_of(moment[:, :ch].astype(BF16), "dp"))

    shape = inputs.shape
    return (out.reshape(shape), xgrad.reshape(shape), p_factor.T, q_factor.T, new_feedback[None])


def solution(mesh):
    in_specs = (
        P("dp", None, "tile", None),
        P(),
        P("dp", None, "tile", None),
        P("dp", "tile", None),
        P(),
    )
    out_specs = (
        P("dp", None, "tile", None),
        P("dp", None, "tile", None),
        P("tile", None),
        P(),
        P("dp", "tile", None),
    )
    return jax.shard_map(
        per_device, mesh=mesh, in_specs=in_specs, out_specs=out_specs, check_vma=False
    )
```

```python
import functools
import math

import jax
import jax.numpy as jnp
from jax import lax
from jax.experimental import pallas as pl
from jax.experimental.pallas import tpu as pltpu
from jax.sharding import PartitionSpec as P

F32 = jnp.float32
BF16 = jnp.bfloat16
NN = (((1,), (0,)), ((), ()))
NT = (((1,), (1,)), ((), ()))
TN = (((0,), (0,)), ((), ()))
VMEM = pl.BlockSpec(memory_space=pltpu.VMEM)
HBM = pl.BlockSpec(memory_space=pl.ANY)
BIG = 24 * 2**20
WHOLE = 56 * 2**20


def dot(left, right, dims=NN):
    return lax.dot_general(left, right, dims, preferred_element_type=F32)


def in_parts(value):
    parts = []
    for _ in range(3):
        part = value.astype(BF16)
        parts.append(part)
        value = value - part.astype(F32)
    return parts


def stacked_parts(value):
    return jnp.concatenate([part.astype(F32) for part in in_parts(value)], 0).astype(BF16)


def fold(product, rank):
    return product[0:rank] + product[rank : 2 * rank] + product[2 * rank : 3 * rank]


def fetch(pairs, sems):
    copies = [pltpu.make_async_copy(held, place, sems.at[k]) for k, (held, place) in enumerate(pairs)]
    for copy in copies:
        copy.start()
    return copies


def swish(preact, upstream):
    s = jax.nn.sigmoid(preact)
    return preact * s, upstream * s * (1.0 + preact * (1.0 - s))


def widen(source, left, right, wide, lat, lon, low, high):
    ch = source.shape[1]
    rows = 8 * lon
    column = lax.broadcasted_iota(jnp.int32, (rows, ch), 0) & (lon - 1)
    wide[0:lon, :] = jnp.zeros((lon, 3 * ch), BF16)
    wide[lon + lat * lon :, :] = jnp.zeros((lon, 3 * ch), BF16)
    for step in range(lat // 8):
        value = source[step * rows : (step + 1) * rows, :]
        wider = value.astype(F32)
        edges = [spread(edge, step, lon) for edge in (left, right)]
        west = jnp.where(column == 0, edges[0], pltpu.roll(wider, 1, 0))
        east = jnp.where(column == lon - 1, edges[1], pltpu.roll(wider, rows - 1, 0))
        at = slice(lon + step * rows, lon + (step + 1) * rows)
        wide[at, low * ch : (low + 1) * ch] = west.astype(BF16)
        wide[at, ch : 2 * ch] = value
        wide[at, high * ch : (high + 1) * ch] = east.astype(BF16)


def spread(edge, step, lon):
    if edge is None:
        return 0.0
    ch = edge.shape[1]
    part = edge[step * 8 : step * 8 + 8, None, :]
    return jnp.broadcast_to(part, (8, lon, ch)).reshape(8 * lon, ch)


def picked(columns, source, lat, lon):
    shape = (lat * len(columns), lat * lon)
    cell = lax.broadcasted_iota(jnp.int32, shape, 1)
    row = lax.broadcasted_iota(jnp.int32, shape, 0)
    target = (row & (lat - 1)) * lon
    for k, column in enumerate(columns):
        target = jnp.where((row >= k * lat) & (row < (k + 1) * lat), target + column, target)
    return dot((cell == target).astype(F32).astype(BF16), source[...]).astype(BF16)


def load_kernel(
    lat, lon, x_hbm, cot_hbm, w_hbm, x_ref, cot_ref, w_ref, east_ref, west_ref, sems
):
    x_copy, cot_copy, w_copy = fetch([(x_hbm, x_ref), (cot_hbm, cot_ref), (w_hbm, w_ref)], sems)
    x_copy.wait()
    x_edge = picked((0, 1, lon - 2, lon - 1), x_ref, lat, lon)
    west_ref[0] = x_edge[0:lat]
    west_ref[1] = x_edge[lat : 2 * lat]
    east_ref[0] = x_edge[2 * lat : 3 * lat]
    east_ref[1] = x_edge[3 * lat : 4 * lat]
    cot_copy.wait()
    cot_edge = picked((0, lon - 1), cot_ref, lat, lon)
    west_ref[2] = cot_edge[0:lat]
    east_ref[2] = cot_edge[lat : 2 * lat]
    w_copy.wait()


def inner_kernel(lat, lon, x_ref, w_ref, x_wide, preact_ref):
    cells, ch = x_ref.shape
    chunk = cells // 2
    widen(x_ref, None, None, x_wide, lat, lon, 0, 2)

    def forward(step, carry):
        at = pl.multiple_of(step * chunk, chunk)
        total = dot(x_wide[pl.ds(at, chunk), :], w_ref[0 : 3 * ch, :])
        total += dot(x_wide[pl.ds(at + lon, chunk), :], w_ref[3 * ch : 6 * ch, :])
        total += dot(x_wide[pl.ds(at + 2 * lon, chunk), :], w_ref[6 * ch : 9 * ch, :])
        preact_ref[pl.ds(at, chunk), :] = total
        return carry

    lax.fori_loop(0, cells // chunk, forward, 0)


def shifted(west, east, lat):
    value = jnp.concatenate([west.astype(F32), east.astype(F32)], 0)
    row = lax.broadcasted_iota(jnp.int32, value.shape, 0) & (lat - 1)
    south = jnp.where(row == 0, 0.0, pltpu.roll(value, 1, 0))
    north = jnp.where(row == lat - 1, 0.0, pltpu.roll(value, 2 * lat - 1, 0))
    return [south.astype(BF16), value.astype(BF16), north.astype(BF16)]


def conv_kernel(
    lat, lon, scale, x_wide, preact_ref, cot_ref, w_ref, left_ref, right_ref,
    out_ref, slope_ref, keep_ref, send_ref, x_sides, wgrad_ref,
):
    cells, ch = cot_ref.shape
    core = lax.axis_index("tile") & 1
    tap = lambda k: w_ref[k * ch : (k + 1) * ch, :]

    beside = shifted(left_ref[1], right_ref[0], lat)

    west = sum(dot(beside[a][0:lat], tap(3 * a)) for a in range(3))
    east = sum(dot(beside[a][lat : 2 * lat], tap(3 * a + 2)) for a in range(3))
    rows = 8 * lon
    column = lax.broadcasted_iota(jnp.int32, (rows, ch), 0) & (lon - 1)
    for step in range(lat // 8):
        at = slice(step * rows, (step + 1) * rows)
        preact = preact_ref[at, :]
        preact += jnp.where(column == 0, spread(west, step, lon), 0.0)
        preact += jnp.where(column == lon - 1, spread(east, step, lon), 0.0)
        out, slope = swish(preact, cot_ref[at, :].astype(F32))
        out_ref[at, :] = out.astype(BF16)
        slope_ref[at, :] = slope.astype(BF16)
        wide_at = slice(lon + step * rows, lon + (step + 1) * rows)
        for side, place, edge in ((0, 0, left_ref[1]), (1, lon - 1, right_ref[0])):
            value = x_wide[wide_at, 2 * side * ch : (2 * side + 1) * ch].astype(F32)
            value = jnp.where(column == place, spread(edge.astype(F32), step, lon), value)
            x_sides[wide_at, side * ch : (side + 1) * ch] = value.astype(BF16)
    x_sides[0:lon, :] = jnp.zeros((lon, 2 * ch), BF16)
    x_sides[lon + cells :, :] = jnp.zeros((lon, 2 * ch), BF16)

    for k in range(9):
        a, b = k // 3, k % 3
        source, block = (x_wide, 1) if b == 1 else (x_sides, b // 2)
        term = dot(
            source[a * lon : a * lon + cells, block * ch : (block + 1) * ch], slope_ref[...], TN
        )
        wgrad_ref[k * ch : (k + 1) * ch, :] = (term * scale).astype(BF16)
    pairs, piece, _ = keep_ref.shape

    def divide(own):
        for place, chip in enumerate(ring_order(pairs)):
            for held, owner in ((keep_ref, own), (send_ref, 1 - own)):
                start = (2 * chip + owner) * piece
                held[place] = wgrad_ref[start : start + piece, :]

    for own in range(2):
        pl.when(core == own)(functools.partial(divide, own))


def conv_call(x, upstream, kernel, lat, lon, tiles, rows_dev, scale):
    cells, ch = x.shape
    kernel_rows = kernel.shape[0]
    sds, local = jax.ShapeDtypeStruct, pltpu.VMEM
    image = local((cells, ch), BF16)
    edges = local((3, lat, ch), BF16)
    x, upstream, kernel, east, west = pl.pallas_call(
        functools.partial(load_kernel, lat, lon),
        out_shape=(image, image, local((kernel_rows, ch), BF16), edges, edges),
        in_specs=[HBM] * 3,
        out_specs=(VMEM,) * 5,
        scratch_shapes=[pltpu.SemaphoreType.DMA((3,))],
        compiler_params=pltpu.CompilerParams(vmem_limit_bytes=WHOLE),
        name="load",
    )(x, upstream, kernel)
    left = lax.ppermute(east, "tile", shift("tile", 1))
    right = lax.ppermute(west, "tile", shift("tile", -1))
    wide, preact = pl.pallas_call(
        functools.partial(inner_kernel, lat, lon),
        out_shape=(local((cells + 2 * lon, 3 * ch), BF16), local((cells, ch), F32)),
        in_specs=[VMEM] * 2,
        out_specs=(VMEM,) * 2,
        compiler_params=pltpu.CompilerParams(vmem_limit_bytes=BIG),
        cost_estimate=pl.CostEstimate(
            flops=2 * cells * kernel_rows * ch, bytes_accessed=0, transcendentals=0
        ),
        name="inner",
    )(x, kernel)
    half = local((tiles // 2, rows_dev, ch), BF16)
    out, slope, keep, send = pl.pallas_call(
        functools.partial(conv_kernel, lat, lon, scale),
        out_shape=(image, image, half, half),
        in_specs=[VMEM] * 6,
        out_specs=(VMEM,) * 4,
        scratch_shapes=[
            pltpu.VMEM((cells + 2 * lon, 2 * ch), BF16),
            pltpu.VMEM((kernel_rows, ch), BF16),
        ],
        compiler_params=pltpu.CompilerParams(vmem_limit_bytes=BIG),
        cost_estimate=pl.CostEstimate(
            flops=2 * cells * kernel_rows * ch, bytes_accessed=2**20, transcendentals=cells * ch
        ),
        name="conv",
    )(wide, preact, upstream, kernel, left, right)
    return out, slope, keep, send, (kernel, east, west, left, right)


def input_grad_kernel(
    lat, lon, out_ref, slope_ref, w_ref, east_ref, west_ref, left_ref, right_ref, out_hbm, xgrad_ref,
    s_wide, out_sem,
):
    cells, ch = slope_ref.shape
    out_copy = pltpu.make_async_copy(out_ref, out_hbm, out_sem)
    out_copy.start()
    chunk = cells // 2
    columns = [
        shifted(left_ref[0], east_ref[1], lat),
        shifted(left_ref[1], right_ref[0], lat),
        shifted(west_ref[0], right_ref[1], lat),
    ]
    total = jnp.zeros((2 * lat, ch), F32)
    for a in range(3):
        for b in range(3):
            tap = 3 * a + b
            total += dot(columns[b][a], w_ref[tap * ch : (tap + 1) * ch, :])
    upstream = jnp.concatenate([left_ref[2].astype(F32), right_ref[2].astype(F32)], 0)
    edge = swish(total, upstream)[1].astype(BF16).astype(F32)
    widen(slope_ref, edge[:lat], edge[lat:], s_wide, lat, lon, 2, 0)

    def input_grad(step, carry):
        at = pl.multiple_of(step * chunk, chunk)
        total = None
        for a in range(3):
            for b in range(3):
                tap = 3 * a + b
                term = dot(
                    s_wide[pl.ds(at + (2 - a) * lon, chunk), b * ch : (b + 1) * ch],
                    w_ref[tap * ch : (tap + 1) * ch, :],
                    NT,
                )
                total = term if total is None else total + term
        xgrad_ref[pl.ds(at, chunk), :] = total.astype(BF16)
        return carry

    lax.fori_loop(0, cells // chunk, input_grad, 0)
    out_copy.wait()


def matrix_kernel(wgrad_ref, error_ref, q_ref, matrix_ref, p_ref):
    matrix = wgrad_ref[0].astype(F32)
    for t in range(1, wgrad_ref.shape[0]):
        matrix += wgrad_ref[t].astype(F32)
    matrix += error_ref[...]
    matrix_ref[...] = matrix
    q_parts = stacked_parts(q_ref[...])
    p_rows = jnp.zeros(p_ref.shape, F32)
    for part in in_parts(matrix):
        p_rows += fold(dot(q_parts, part, NT), q_ref.shape[0])
    p_ref[...] = p_rows.astype(BF16)


def image_mean(ref):
    total = ref[0].astype(F32)
    for image in range(1, ref.shape[0]):
        total += ref[image].astype(F32)
    return total * (1.0 / ref.shape[0])


def moment_kernel(matrix_ref, p_ref, rows_ref, moment_ref):
    _, rank, rows = p_ref.shape
    ch = matrix_ref.shape[1]
    p_rows = image_mean(p_ref)
    rows_ref[...] = p_rows
    p_parts = stacked_parts(p_rows)
    moment = jnp.zeros((rank, ch), F32)
    for part in in_parts(matrix_ref[...]):
        moment += fold(dot(p_parts, part), rank)
    moment_ref[:, 0:ch] = moment.astype(BF16)
    gram = jnp.zeros((rank, 128), F32)
    for part in in_parts(p_rows):
        thrice = [part.astype(F32)] * 3 + [jnp.zeros((128 - 3 * rank, rows), F32)]
        gram += fold(dot(p_parts, jnp.concatenate(thrice, 0).astype(BF16), NT), rank)
    place = lax.broadcasted_iota(jnp.int32, (rank, 128), 1) // rank
    parts = [part.astype(F32) for part in in_parts(gram)]
    parts = jnp.where(place == 0, parts[0], jnp.where(place == 1, parts[1], parts[2]))
    moment_ref[:, ch : ch + 128] = parts.astype(BF16)


def factor_kernel(gram_ref, p_ref, left_ref, columns_ref, solve_ref):
    rank = p_ref.shape[0]
    gram = gram_ref[...]
    gram += pltpu.roll(gram, 128 - rank, 1) + pltpu.roll(gram, 128 - 2 * rank, 1)
    whole = gram
    p_rows = p_ref[...]
    index = lax.broadcasted_iota(jnp.int32, (rank, 1), 0)
    lane = lax.broadcasted_iota(jnp.int32, (rank, 128), 1)
    solve = jnp.where(lane == index, 1.0, 0.0)
    for j in range(rank):
        floor = 1e-14 * whole[j : j + 1, j : j + 1]
        inverse = 1.0 / jnp.sqrt(jnp.maximum(gram[j : j + 1, j : j + 1], floor))
        projected = jnp.where(index > j, gram[:, j : j + 1] * inverse, 0.0)

        def step(value):
            unit = value[j : j + 1, :] * inverse
            return jnp.where(index == j, unit, value - projected * unit)

        gram, p_rows, solve = step(gram), step(p_rows), step(solve)
    left_ref[...] = p_rows
    columns_ref[...] = p_rows.T
    solve_ref[...] = solve


def residual_kernel(matrix_ref, columns_ref, solve_ref, s_ref, next_ref, right_ref):
    rank = s_ref.shape[1]
    mean = image_mean(s_ref)
    solve = solve_ref[...]
    right = solve[:, 0:1] * mean[0:1, :]
    for k in range(1, rank):
        right += solve[:, k : k + 1] * mean[k : k + 1, :]
    right_ref[...] = right
    columns = columns_ref[...]
    total = matrix_ref[...]
    for k in range(rank):
        total -= columns[:, k : k + 1] * right[k : k + 1, :]
    next_ref[...] = total


def shift(axis, step):
    count = lax.axis_size(axis)
    return [(i, (i + step) % count) for i in range(count)]


def cores(axis):
    return [(i, i ^ 1) for i in range(lax.axis_size(axis))]


def ring_order(count):
    order, step = [0], count
    while len(order) < count:
        step //= 2
        order += [chip + step for chip in order]
    return order


def chips(axis):
    order = ring_order(lax.axis_size(axis) // 2)
    return [[2 * chip + core for chip in order] for core in range(2)]


def shares_of(value, axis):
    count = lax.axis_size(axis)
    return lax.all_to_all(
        jnp.broadcast_to(value[None], (count,) + value.shape), axis, 0, 0, tiled=True
    )


def per_device(inputs, kernel, cotangent, feedback, q_start):
    _, lat, lon, ch = inputs.shape
    kernel_rows = kernel.shape[0]
    rows_dev = feedback.shape[1]
    rank = q_start.shape[1]
    cells = lat * lon
    tiles = lax.axis_size("tile")
    scale = 1.0 / math.sqrt(cells * tiles)
    x, upstream, error = inputs[0], cotangent[0], feedback[0]

    x_cells, upstream_cells = x.reshape(cells, ch), upstream.reshape(cells, ch)
    sds, local = jax.ShapeDtypeStruct, pltpu.VMEM
    out, slope, keep, send, held = conv_call(
        x_cells, upstream_cells, kernel, lat, lon, tiles, rows_dev, scale
    )
    out, xgrad = pl.pallas_call(
        functools.partial(input_grad_kernel, lat, lon),
        out_shape=(sds((cells, ch), BF16),) * 2,
        in_specs=[VMEM] * 7,
        out_specs=(HBM, VMEM),
        scratch_shapes=[
            pltpu.VMEM((cells + 2 * lon, 3 * ch), BF16),
            pltpu.SemaphoreType.DMA,
        ],
        compiler_params=pltpu.CompilerParams(vmem_limit_bytes=BIG),
        cost_estimate=pl.CostEstimate(
            flops=2 * cells * kernel_rows * ch, bytes_accessed=2 * 2**20, transcendentals=0
        ),
        name="input_grad",
    )(out, slope, *held)

    summed = keep + lax.ppermute(send, "tile", cores("tile"))
    wgrad_rows = lax.all_to_all(
        summed, "tile", 0, 0, axis_index_groups=chips("tile"), tiled=True
    )
    small = pltpu.CompilerParams(vmem_limit_bytes=16 * 2**20)
    matrix, p_local = pl.pallas_call(
        matrix_kernel,
        out_shape=(local((rows_dev, ch), F32), local((rank, rows_dev), BF16)),
        in_specs=[VMEM] * 3,
        out_specs=(VMEM,) * 2,
        compiler_params=small,
        name="matrix",
    )(wgrad_rows, error, q_start.T)
    p_rows, moment = pl.pallas_call(
        moment_kernel,
        out_shape=(local((rank, rows_dev), F32), local((rank, ch + 128), BF16)),
        in_specs=[VMEM] * 2,
        out_specs=(VMEM,) * 2,
        compiler_params=small,
        name="moment",
    )(matrix, shares_of(p_local, "dp"))
    moment = shares_of(moment, "tile").astype(F32).sum(0)
    p_factor, columns, solve = pl.pallas_call(
        factor_kernel,
        out_shape=(
            sds((rank, rows_dev), F32),
            local((rows_dev, rank), F32),
            local((rank, 128), F32),
        ),
        in_specs=[VMEM] * 2,
        out_specs=(VMEM,) * 3,
        compiler_params=small,
        name="factor",
    )(moment[:, ch:], p_rows)
    new_feedback, q_factor = pl.pallas_call(
        residual_kernel,
        out_shape=(sds((rows_dev, ch), F32), sds((rank, ch), F32)),
        in_specs=[VMEM] * 4,
        out_specs=(VMEM,) * 2,
        compiler_params=small,
        name="residual",
    )(matrix, columns, solve, shares_of(moment[:, :ch].astype(BF16), "dp"))

    shape = inputs.shape
    return (out.reshape(shape), xgrad.reshape(shape), p_factor.T, q_factor.T, new_feedback[None])


def solution(mesh):
    in_specs = (
        P("dp", None, "tile", None),
        P(),
        P("dp", None, "tile", None),
        P("dp", "tile", None),
        P(),
    )
    out_specs = (
        P("dp", None, "tile", None),
        P("dp", None, "tile", None),
        P("tile", None),
        P(),
        P("dp", "tile", None),
    )
    return jax.shard_map(
        per_device, mesh=mesh, in_specs=in_specs, out_specs=out_specs, check_vma=False
    )
```

```python
import functools
import math

import jax
import jax.numpy as jnp
from jax import lax
from jax.experimental import pallas as pl
from jax.experimental.pallas import tpu as pltpu
from jax.sharding import PartitionSpec as P

F32 = jnp.float32
BF16 = jnp.bfloat16
NN = (((1,), (0,)), ((), ()))
NT = (((1,), (1,)), ((), ()))
TN = (((0,), (0,)), ((), ()))
VMEM = pl.BlockSpec(memory_space=pltpu.VMEM)
HBM = pl.BlockSpec(memory_space=pl.ANY)
BIG = 24 * 2**20
WHOLE = 56 * 2**20


def dot(left, right, dims=NN):
    return lax.dot_general(left, right, dims, preferred_element_type=F32)


def in_parts(value):
    parts = []
    for _ in range(3):
        part = value.astype(BF16)
        parts.append(part)
        value = value - part.astype(F32)
    return parts


def stacked_parts(value):
    return jnp.concatenate([part.astype(F32) for part in in_parts(value)], 0).astype(BF16)


def fold(product, rank):
    return product[0:rank] + product[rank : 2 * rank] + product[2 * rank : 3 * rank]


def fetch(pairs, sems):
    copies = [pltpu.make_async_copy(held, place, sems.at[k]) for k, (held, place) in enumerate(pairs)]
    for copy in copies:
        copy.start()
    return copies


def swish(preact, upstream):
    s = jax.nn.sigmoid(preact)
    return preact * s, upstream * s * (1.0 + preact * (1.0 - s))


def widen(source, left, right, wide, lat, lon, low, high):
    ch = source.shape[1]
    rows = 8 * lon
    column = lax.broadcasted_iota(jnp.int32, (rows, ch), 0) & (lon - 1)
    wide[0:lon, :] = jnp.zeros((lon, 3 * ch), BF16)
    wide[lon + lat * lon :, :] = jnp.zeros((lon, 3 * ch), BF16)
    for step in range(lat // 8):
        value = source[step * rows : (step + 1) * rows, :]
        wider = value.astype(F32)
        edges = [spread(edge, step, lon) for edge in (left, right)]
        west = jnp.where(column == 0, edges[0], pltpu.roll(wider, 1, 0))
        east = jnp.where(column == lon - 1, edges[1], pltpu.roll(wider, rows - 1, 0))
        at = slice(lon + step * rows, lon + (step + 1) * rows)
        wide[at, low * ch : (low + 1) * ch] = west.astype(BF16)
        wide[at, ch : 2 * ch] = value
        wide[at, high * ch : (high + 1) * ch] = east.astype(BF16)


def spread(edge, step, lon):
    if edge is None:
        return 0.0
    ch = edge.shape[1]
    part = edge[step * 8 : step * 8 + 8, None, :]
    return jnp.broadcast_to(part, (8, lon, ch)).reshape(8 * lon, ch)


def picked(columns, source, lat, lon):
    shape = (lat * len(columns), lat * lon)
    cell = lax.broadcasted_iota(jnp.int32, shape, 1)
    row = lax.broadcasted_iota(jnp.int32, shape, 0)
    target = (row & (lat - 1)) * lon
    for k, column in enumerate(columns):
        target = jnp.where((row >= k * lat) & (row < (k + 1) * lat), target + column, target)
    return dot((cell == target).astype(F32).astype(BF16), source[...]).astype(BF16)


def load_kernel(
    lat, lon, x_hbm, cot_hbm, w_hbm, x_ref, cot_ref, w_ref, east_ref, west_ref, sems
):
    x_copy, cot_copy, w_copy = fetch([(x_hbm, x_ref), (cot_hbm, cot_ref), (w_hbm, w_ref)], sems)
    x_copy.wait()
    x_edge = picked((0, 1, lon - 2, lon - 1), x_ref, lat, lon)
    west_ref[0] = x_edge[0:lat]
    west_ref[1] = x_edge[lat : 2 * lat]
    east_ref[0] = x_edge[2 * lat : 3 * lat]
    east_ref[1] = x_edge[3 * lat : 4 * lat]
    cot_copy.wait()
    cot_edge = picked((0, lon - 1), cot_ref, lat, lon)
    west_ref[2] = cot_edge[0:lat]
    east_ref[2] = cot_edge[lat : 2 * lat]
    w_copy.wait()


def inner_kernel(lat, lon, x_ref, w_ref, x_wide, preact_ref):
    cells, ch = x_ref.shape
    chunk = cells // 2
    widen(x_ref, None, None, x_wide, lat, lon, 0, 2)

    def forward(step, carry):
        at = pl.multiple_of(step * chunk, chunk)
        total = dot(x_wide[pl.ds(at, chunk), :], w_ref[0 : 3 * ch, :])
        total += dot(x_wide[pl.ds(at + lon, chunk), :], w_ref[3 * ch : 6 * ch, :])
        total += dot(x_wide[pl.ds(at + 2 * lon, chunk), :], w_ref[6 * ch : 9 * ch, :])
        preact_ref[pl.ds(at, chunk), :] = total
        return carry

    lax.fori_loop(0, cells // chunk, forward, 0)


def shifted(west, east, lat):
    value = jnp.concatenate([west.astype(F32), east.astype(F32)], 0)
    row = lax.broadcasted_iota(jnp.int32, value.shape, 0) & (lat - 1)
    south = jnp.where(row == 0, 0.0, pltpu.roll(value, 1, 0))
    north = jnp.where(row == lat - 1, 0.0, pltpu.roll(value, 2 * lat - 1, 0))
    return [south.astype(BF16), value.astype(BF16), north.astype(BF16)]


def conv_kernel(
    lat, lon, scale, x_wide, preact_ref, cot_ref, w_ref, left_ref, right_ref,
    out_ref, slope_ref, keep_ref, send_ref, x_sides, wgrad_ref,
):
    cells, ch = cot_ref.shape
    core = lax.axis_index("tile") & 1
    tap = lambda k: w_ref[k * ch : (k + 1) * ch, :]

    beside = shifted(left_ref[1], right_ref[0], lat)

    west = sum(dot(beside[a][0:lat], tap(3 * a)) for a in range(3))
    east = sum(dot(beside[a][lat : 2 * lat], tap(3 * a + 2)) for a in range(3))
    rows = 8 * lon
    column = lax.broadcasted_iota(jnp.int32, (rows, ch), 0) & (lon - 1)
    for step in range(lat // 8):
        at = slice(step * rows, (step + 1) * rows)
        preact = preact_ref[at, :]
        preact += jnp.where(column == 0, spread(west, step, lon), 0.0)
        preact += jnp.where(column == lon - 1, spread(east, step, lon), 0.0)
        out, slope = swish(preact, cot_ref[at, :].astype(F32))
        out_ref[at, :] = out.astype(BF16)
        slope_ref[at, :] = slope.astype(BF16)
        wide_at = slice(lon + step * rows, lon + (step + 1) * rows)
        for side, place, edge in ((0, 0, left_ref[1]), (1, lon - 1, right_ref[0])):
            value = x_wide[wide_at, 2 * side * ch : (2 * side + 1) * ch].astype(F32)
            value = jnp.where(column == place, spread(edge.astype(F32), step, lon), value)
            x_sides[wide_at, side * ch : (side + 1) * ch] = value.astype(BF16)
    x_sides[0:lon, :] = jnp.zeros((lon, 2 * ch), BF16)
    x_sides[lon + cells :, :] = jnp.zeros((lon, 2 * ch), BF16)

    for k in range(9):
        a, b = k // 3, k % 3
        source, block = (x_wide, 1) if b == 1 else (x_sides, b // 2)
        term = dot(
            source[a * lon : a * lon + cells, block * ch : (block + 1) * ch], slope_ref[...], TN
        )
        wgrad_ref[k * ch : (k + 1) * ch, :] = (term * scale).astype(BF16)
    pairs, piece, _ = keep_ref.shape

    def divide(own):
        for place, chip in enumerate(ring_order(pairs)):
            for held, owner in ((keep_ref, own), (send_ref, 1 - own)):
                start = (2 * chip + owner) * piece
                held[place] = wgrad_ref[start : start + piece, :]

    for own in range(2):
        pl.when(core == own)(functools.partial(divide, own))


def conv_call(x, upstream, kernel, lat, lon, tiles, rows_dev, scale):
    cells, ch = x.shape
    kernel_rows = kernel.shape[0]
    sds, local = jax.ShapeDtypeStruct, pltpu.VMEM
    image = local((cells, ch), BF16)
    edges = local((3, lat, ch), BF16)
    x, upstream, kernel, east, west = pl.pallas_call(
        functools.partial(load_kernel, lat, lon),
        out_shape=(image, image, local((kernel_rows, ch), BF16), edges, edges),
        in_specs=[HBM] * 3,
        out_specs=(VMEM,) * 5,
        scratch_shapes=[pltpu.SemaphoreType.DMA((3,))],
        compiler_params=pltpu.CompilerParams(vmem_limit_bytes=WHOLE),
        name="load",
    )(x, upstream, kernel)
    left = lax.ppermute(east, "tile", shift("tile", 1))
    right = lax.ppermute(west, "tile", shift("tile", -1))
    wide, preact = pl.pallas_call(
        functools.partial(inner_kernel, lat, lon),
        out_shape=(local((cells + 2 * lon, 3 * ch), BF16), local((cells, ch), F32)),
        in_specs=[VMEM] * 2,
        out_specs=(VMEM,) * 2,
        compiler_params=pltpu.CompilerParams(vmem_limit_bytes=BIG),
        cost_estimate=pl.CostEstimate(
            flops=2 * cells * kernel_rows * ch, bytes_accessed=0, transcendentals=0
        ),
        name="inner",
    )(x, kernel)
    half = local((tiles // 2, rows_dev, ch), BF16)
    out, slope, keep, send = pl.pallas_call(
        functools.partial(conv_kernel, lat, lon, scale),
        out_shape=(image, image, half, half),
        in_specs=[VMEM] * 6,
        out_specs=(VMEM,) * 4,
        scratch_shapes=[
            pltpu.VMEM((cells + 2 * lon, 2 * ch), BF16),
            pltpu.VMEM((kernel_rows, ch), BF16),
        ],
        compiler_params=pltpu.CompilerParams(vmem_limit_bytes=BIG),
        cost_estimate=pl.CostEstimate(
            flops=2 * cells * kernel_rows * ch, bytes_accessed=2**20, transcendentals=cells * ch
        ),
        name="conv",
    )(wide, preact, upstream, kernel, left, right)
    return out, slope, keep, send, (kernel, east, west, left, right)


def input_grad_kernel(
    lat, lon, out_ref, slope_ref, w_ref, east_ref, west_ref, left_ref, right_ref, out_hbm, xgrad_ref,
    s_wide, out_sem,
):
    cells, ch = slope_ref.shape
    out_copy = pltpu.make_async_copy(out_ref, out_hbm, out_sem)
    out_copy.start()
    chunk = cells // 2
    columns = [
        shifted(left_ref[0], east_ref[1], lat),
        shifted(left_ref[1], right_ref[0], lat),
        shifted(west_ref[0], right_ref[1], lat),
    ]
    total = jnp.zeros((2 * lat, ch), F32)
    for a in range(3):
        for b in range(3):
            tap = 3 * a + b
            total += dot(columns[b][a], w_ref[tap * ch : (tap + 1) * ch, :])
    upstream = jnp.concatenate([left_ref[2].astype(F32), right_ref[2].astype(F32)], 0)
    edge = swish(total, upstream)[1].astype(BF16).astype(F32)
    widen(slope_ref, edge[:lat], edge[lat:], s_wide, lat, lon, 2, 0)

    def input_grad(step, carry):
        at = pl.multiple_of(step * chunk, chunk)
        total = None
        for a in range(3):
            for b in range(3):
                tap = 3 * a + b
                term = dot(
                    s_wide[pl.ds(at + (2 - a) * lon, chunk), b * ch : (b + 1) * ch],
                    w_ref[tap * ch : (tap + 1) * ch, :],
                    NT,
                )
                total = term if total is None else total + term
        xgrad_ref[pl.ds(at, chunk), :] = total.astype(BF16)
        return carry

    lax.fori_loop(0, cells // chunk, input_grad, 0)
    out_copy.wait()


def matrix_kernel(wgrad_ref, error_ref, q_ref, matrix_ref, p_ref):
    matrix = wgrad_ref[0].astype(F32)
    for t in range(1, wgrad_ref.shape[0]):
        matrix += wgrad_ref[t].astype(F32)
    matrix += error_ref[...]
    matrix_ref[...] = matrix
    q_parts = stacked_parts(q_ref[...])
    p_rows = jnp.zeros(p_ref.shape, F32)
    for part in in_parts(matrix):
        p_rows += fold(dot(q_parts, part, NT), q_ref.shape[0])
    p_ref[...] = p_rows.astype(BF16)


def image_mean(ref):
    total = ref[0].astype(F32)
    for image in range(1, ref.shape[0]):
        total += ref[image].astype(F32)
    return total * (1.0 / ref.shape[0])


def moment_kernel(matrix_ref, p_ref, rows_ref, moment_ref):
    _, rank, rows = p_ref.shape
    ch = matrix_ref.shape[1]
    p_rows = image_mean(p_ref)
    rows_ref[...] = p_rows
    p_parts = stacked_parts(p_rows)
    moment = jnp.zeros((rank, ch), F32)
    for part in in_parts(matrix_ref[...]):
        moment += fold(dot(p_parts, part), rank)
    moment_ref[:, 0:ch] = moment.astype(BF16)
    gram = jnp.zeros((rank, 128), F32)
    for part in in_parts(p_rows):
        thrice = [part.astype(F32)] * 3 + [jnp.zeros((128 - 3 * rank, rows), F32)]
        gram += fold(dot(p_parts, jnp.concatenate(thrice, 0).astype(BF16), NT), rank)
    place = lax.broadcasted_iota(jnp.int32, (rank, 128), 1) // rank
    parts = [part.astype(F32) for part in in_parts(gram)]
    parts = jnp.where(place == 0, parts[0], jnp.where(place == 1, parts[1], parts[2]))
    moment_ref[:, ch : ch + 128] = parts.astype(BF16)


def factor_kernel(gram_ref, p_ref, left_ref, columns_ref, solve_ref):
    rank = p_ref.shape[0]
    gram = gram_ref[...]
    gram += pltpu.roll(gram, 128 - rank, 1) + pltpu.roll(gram, 128 - 2 * rank, 1)
    whole = gram
    p_rows = p_ref[...]
    index = lax.broadcasted_iota(jnp.int32, (rank, 1), 0)
    lane = lax.broadcasted_iota(jnp.int32, (rank, 128), 1)
    solve = jnp.where(lane == index, 1.0, 0.0)
    for j in range(rank):
        floor = 1e-14 * whole[j : j + 1, j : j + 1]
        inverse = 1.0 / jnp.sqrt(jnp.maximum(gram[j : j + 1, j : j + 1], floor))
        projected = jnp.where(index > j, gram[:, j : j + 1] * inverse, 0.0)

        def step(value):
            unit = value[j : j + 1, :] * inverse
            return jnp.where(index == j, unit, value - projected * unit)

        gram, p_rows, solve = step(gram), step(p_rows), step(solve)
    left_ref[...] = p_rows
    columns_ref[...] = p_rows.T
    solve_ref[...] = solve


def residual_kernel(matrix_ref, columns_ref, solve_ref, s_ref, next_ref, right_ref):
    rank = s_ref.shape[1]
    mean = image_mean(s_ref)
    solve = solve_ref[...]
    right = solve[:, 0:1] * mean[0:1, :]
    for k in range(1, rank):
        right += solve[:, k : k + 1] * mean[k : k + 1, :]
    right_ref[...] = right
    columns = columns_ref[...]
    total = matrix_ref[...]
    for k in range(rank):
        total -= columns[:, k : k + 1] * right[k : k + 1, :]
    next_ref[...] = total


def shift(axis, step):
    count = lax.axis_size(axis)
    return [(i, (i + step) % count) for i in range(count)]


def cores(axis):
    return [(i, i ^ 1) for i in range(lax.axis_size(axis))]


def ring_order(count):
    order, step = [0], count
    while len(order) < count:
        step //= 2
        order += [chip + step for chip in order]
    return order


def chips(axis):
    order = ring_order(lax.axis_size(axis) // 2)
    return [[2 * chip + core for chip in order] for core in range(2)]


def shares_of(value, axis):
    count = lax.axis_size(axis)
    return lax.all_to_all(
        jnp.broadcast_to(value[None], (count,) + value.shape),
        axis,
        0,
        0,
        axis_index_groups=[ring_order(count)],
        tiled=True,
    )


def per_device(inputs, kernel, cotangent, feedback, q_start):
    _, lat, lon, ch = inputs.shape
    kernel_rows = kernel.shape[0]
    rows_dev = feedback.shape[1]
    rank = q_start.shape[1]
    cells = lat * lon
    tiles = lax.axis_size("tile")
    scale = 1.0 / math.sqrt(cells * tiles)
    x, upstream, error = inputs[0], cotangent[0], feedback[0]

    x_cells, upstream_cells = x.reshape(cells, ch), upstream.reshape(cells, ch)
    sds, local = jax.ShapeDtypeStruct, pltpu.VMEM
    out, slope, keep, send, held = conv_call(
        x_cells, upstream_cells, kernel, lat, lon, tiles, rows_dev, scale
    )
    out, xgrad = pl.pallas_call(
        functools.partial(input_grad_kernel, lat, lon),
        out_shape=(sds((cells, ch), BF16),) * 2,
        in_specs=[VMEM] * 7,
        out_specs=(HBM, VMEM),
        scratch_shapes=[
            pltpu.VMEM((cells + 2 * lon, 3 * ch), BF16),
            pltpu.SemaphoreType.DMA,
        ],
        compiler_params=pltpu.CompilerParams(vmem_limit_bytes=BIG),
        cost_estimate=pl.CostEstimate(
            flops=2 * cells * kernel_rows * ch, bytes_accessed=2 * 2**20, transcendentals=0
        ),
        name="input_grad",
    )(out, slope, *held)

    summed = keep + lax.ppermute(send, "tile", cores("tile"))
    wgrad_rows = lax.all_to_all(
        summed, "tile", 0, 0, axis_index_groups=chips("tile"), tiled=True
    )
    small = pltpu.CompilerParams(vmem_limit_bytes=16 * 2**20)
    matrix, p_local = pl.pallas_call(
        matrix_kernel,
        out_shape=(local((rows_dev, ch), F32), local((rank, rows_dev), BF16)),
        in_specs=[VMEM] * 3,
        out_specs=(VMEM,) * 2,
        compiler_params=small,
        name="matrix",
    )(wgrad_rows, error, q_start.T)
    p_rows, moment = pl.pallas_call(
        moment_kernel,
        out_shape=(local((rank, rows_dev), F32), local((rank, ch + 128), BF16)),
        in_specs=[VMEM] * 2,
        out_specs=(VMEM,) * 2,
        compiler_params=small,
        name="moment",
    )(matrix, shares_of(p_local, "dp"))
    moment = shares_of(moment, "tile").astype(F32).sum(0)
    p_factor, columns, solve = pl.pallas_call(
        factor_kernel,
        out_shape=(
            sds((rank, rows_dev), F32),
            local((rows_dev, rank), F32),
            local((rank, 128), F32),
        ),
        in_specs=[VMEM] * 2,
        out_specs=(VMEM,) * 3,
        compiler_params=small,
        name="factor",
    )(moment[:, ch:], p_rows)
    new_feedback, q_factor = pl.pallas_call(
        residual_kernel,
        out_shape=(sds((rows_dev, ch), F32), sds((rank, ch), F32)),
        in_specs=[VMEM] * 4,
        out_specs=(VMEM,) * 2,
        compiler_params=small,
        name="residual",
    )(matrix, columns, solve, shares_of(moment[:, :ch].astype(BF16), "dp"))

    shape = inputs.shape
    return (out.reshape(shape), xgrad.reshape(shape), p_factor.T, q_factor.T, new_feedback[None])


def solution(mesh):
    in_specs = (
        P("dp", None, "tile", None),
        P(),
        P("dp", None, "tile", None),
        P("dp", "tile", None),
        P(),
    )
    out_specs = (
        P("dp", None, "tile", None),
        P("dp", None, "tile", None),
        P("tile", None),
        P(),
        P("dp", "tile", None),
    )
    return jax.shard_map(
        per_device, mesh=mesh, in_specs=in_specs, out_specs=out_specs, check_vma=False
    )
```
